32 devices in a mesh: req: 4 (over x, core), tok: 8 (over z, y).
Axes of the slice: x: 2, y: 2, z: 4, core: 2. Of those that a mesh axis runs over, the one named last changes fastest.
Arguments:
- hidden: bfloat16 [4, 1024, 2048], P('req', 'tok'), may hold values from -4 to 4
- queries: bfloat16 [4, 1024, 3072], P('req', 'tok'), may hold values from -18 to 18
- fresh_latent: bfloat16 [4, 1024, 576], P('req', 'tok'), may hold values from -8 to 8
- latent_cache: bfloat16 [4, 8, 128, 576], P('req', 'tok'), may hold values from -8 to 8
- page_table: int32 [4, 8], P('req'), may hold values from 0 to 7, each once within a row
- cache_lengths: int32 [4], P('req'), may hold values from 2 to 1024, as said below
- routes: int32 [4, 1024, 6], P('req', 'tok'), may hold values from 0 to 63, all different within a row; in each aligned block of 128 rows (0 to 127, 128 to 255, ..., all dimensions but the last counted through in order) at most 14 rows name the same one
- route_gates: float32 [4, 1024, 6], P('req', 'tok'), may hold values from 0.05 to 0.45
- kv_up: bfloat16 [512, 4096], replicated, may hold values from -0.25 to 0.25
- out_proj: bfloat16 [2048, 2048], replicated, may hold values from -0.125 to 0.125
- latent_gain: float32 [512], replicated, may hold values from 0.1 to 1.9
- norm_gain: float32 [2048], replicated, may hold values from 0.1 to 1.9
- expert_in: bfloat16 [128, 2048, 1408], P(('req', 'tok')), may hold values from -0.125 to 0.125
- expert_out: bfloat16 [128, 704, 2048], P(('req', 'tok')), may hold values from -0.15625 to 0.15625
Outputs:
- layer_out: bfloat16 [4, 1024, 2048], P('req', 'tok')
- new_latent: bfloat16 [4, 1024, 576], P('req', 'tok')
The draws below stay inside these ranges and needn't reach their ends.
Inputs may be any that keep to these rules, and one draw needn't show every extreme that they name: `page_table`: each request's row names every pool page once. `cache_lengths`: some request has exactly 1024 cached tokens. `routes`: the 6 experts of a token differ; among the rows of one device no expert is named more than 14 times, and that bound is reached.
All inputs are finite; a program needn't handle non-finite values.
Results may differ from the reference program's by a relative error of at most 0.013.
Values may be sent and summed in bfloat16 or wider, within the bound.
No kernel may reach another device: no remote copies, remote signals or barrier semaphores. Data moves between devices by JAX's collectives and lax.ppermute only.
A program may use at most 192 MiB of HBM per device.

```python
import math
import jax
import jax.numpy as jnp
import numpy as np
from jax import lax

D = 2048
H = 16
NOPE = 128
ROPE = 64
VD = 128
LAT = 512
EXPERTS = 64
FF_E = 1408
TOP = 6
TOK_DEV = 128
PAGE = 128
HALF = 704
CAP = 14
REQ = 4
NEW_TOK = 1024
POOL = 8
CTX_MAX = 1024
SLABS = 128
N_REQ = 4
N_TOK = 8


def request_lengths(key):
    first_key, second_key = jax.random.split(jax.random.fold_in(key, 7100))
    values = jax.random.randint(first_key, (REQ,), 2, CTX_MAX + 1)
    longest = jax.random.randint(second_key, (), 0, REQ)
    return jnp.where(jnp.arange(REQ) == longest, CTX_MAX, values).astype(jnp.int32)


def draw_cache_lengths(key, part):
    return request_lengths(key)


def background_values(key, shape):
    return jnp.clip(jax.random.normal(key, shape, jnp.float32), -6.0, 6.0)


def planted_pattern(key):
    sign_key, level_key = jax.random.split(jax.random.fold_in(key, 7001))
    half_rope = ROPE // 2
    pair_count = ROPE // 4
    column = jnp.arange(ROPE, dtype=jnp.int32)
    planted_column = column % half_rope >= half_rope - pair_count
    signs = (2 * jax.random.randint(sign_key, (REQ, ROPE), 0, 2) - 1).astype(jnp.float32)
    signs = jnp.where(column == half_rope - 1, 1.0, jnp.where(column == ROPE - 1, -1.0, signs))
    token = jnp.arange(NEW_TOK, dtype=jnp.int32)
    planted_row = token % 8 == 7
    levels = (8 + 2 * jax.random.randint(level_key, (REQ, NEW_TOK, H), 0, 3)).astype(jnp.float32)
    first_spot = (jnp.arange(REQ)[:, None, None] == 0) & (token[None, :, None] == 7) & (jnp.arange(H)[None, None, :] == 0)
    levels = jnp.where(first_spot, 12.0, levels)
    return (planted_column, signs, planted_row, levels)


def draw_fresh_latent(key, part):
    background = background_values(jax.random.fold_in(key, 7002), (REQ, NEW_TOK, LAT + ROPE))
    return background.astype(jnp.bfloat16)


def draw_latent_cache(key, part):
    planted_column, signs, planted_row, levels = planted_pattern(key)
    background = background_values(jax.random.fold_in(key, 7004), (REQ, POOL, PAGE, LAT + ROPE))
    row = jnp.arange(PAGE, dtype=jnp.int32)
    magnitude = jnp.where(row == 0, 8.0, jnp.where(row == 1, 7.9375, 0.0))
    picked = (row < 2)[:, None] & planted_column[None, :]
    planted = magnitude[None, None, :, None] * signs[:, None, None, :]
    rope_part = jnp.where(picked[None, None, :, :], planted, background[..., LAT:])
    return jnp.concatenate([background[..., :LAT], rope_part], axis=-1).astype(jnp.bfloat16)


def draw_queries(key, part):
    planted_column, signs, planted_row, levels = planted_pattern(key)
    lengths = request_lengths(key)
    background = background_values(jax.random.fold_in(key, 7003), (REQ, NEW_TOK, H, NOPE + ROPE))
    multiplier = max(1, 32 // ROPE)
    half_rope = ROPE // 2
    frequency = 10000.0 ** (-jnp.arange(half_rope, dtype=jnp.float32) * 2.0 / ROPE)
    positions = lengths[:, None] + jnp.arange(NEW_TOK, dtype=jnp.int32)[None, :]
    angles = positions.astype(jnp.float32)[:, :, None, None] * frequency[None, None, None, :]
    aligned = levels[..., None] * multiplier * signs[:, None, None, :]
    aligned = jnp.where(planted_column, aligned, 0.0)
    front_part = aligned[..., :half_rope]
    back_part = aligned[..., half_rope:]
    cosine = jnp.cos(angles)
    sine_part = jnp.sin(angles)
    turned = jnp.concatenate([front_part * cosine + back_part * sine_part, back_part * cosine - front_part * sine_part], axis=-1)
    row_mask = planted_row[None, :, None, None]
    rope_back = background[..., NOPE:]
    quiet = jnp.where(planted_column, 0.1 * rope_back, rope_back)
    rope_part = jnp.where(row_mask, turned, quiet)
    nope_part = jnp.where(row_mask, 0.0, background[..., :NOPE])
    joined = jnp.concatenate([nope_part, rope_part], axis=-1)
    return joined.reshape(REQ, NEW_TOK, H * (NOPE + ROPE)).astype(jnp.bfloat16)


def shard_levels(stream_key, extent, pieces, smallest, largest):
    def one(position, blocks):
        draws = jax.random.uniform(jax.random.fold_in(jax.random.fold_in(stream_key, 6), position), (blocks,), jnp.float32, smallest / len(pieces), largest / len(pieces))
        return jnp.repeat(jnp.exp(draws), extent[position] // blocks).reshape((-1,) + (1,) * (len(extent) - position - 1))

    level = one(*pieces[0])
    for cut in pieces[1:]:
        level = level * one(*cut)
    return level


def shared_out(stream_key, own, number, rows, amount, top, most, slope):
    order = jax.random.permutation(stream_key, amount)
    heavy_load, usual = shares(amount, rows * top, most, slope, True), shares(amount, rows * top, most, slope, False)
    places = jnp.arange(amount)

    def named(sizes, offset_by):
        used = int((sizes > 0).sum())
        fixed = max(1, used // 4)
        shifted = fixed + (places - fixed + offset_by * (used - fixed)) % max(1, amount - fixed)
        return jnp.zeros((amount,), jnp.int32).at[order[jnp.where(places < fixed, places, shifted)]].set(jnp.asarray(sizes, jnp.int32))

    sizes = jnp.where(number % 4 == 0, named(heavy_load, number // 4), named(usual, number - number // 4 - 1))
    mixed = jax.random.permutation(jax.random.fold_in(own, 3), amount)
    donor, receiver = mixed[0:amount // 2 * 2:2], mixed[1:amount // 2 * 2:2]
    margin = jnp.minimum(sizes[donor] - 1, most - sizes[receiver]) // 2
    margin = jnp.where((donor == order[0]) | (receiver == order[0]) | (sizes[receiver] == 0), 0, jnp.maximum(margin, 0))
    shifted = jax.random.randint(jax.random.fold_in(own, 4), (amount // 2,), 0, 1 << 20) % (margin + 1)
    sizes = sizes.at[donor].add(-shifted).at[receiver].add(shifted)
    items = jnp.searchsorted(jnp.cumsum(sizes), jnp.arange(rows * top), side="right").astype(jnp.int32)
    grid = items.reshape(top, rows).T
    grid = grid[jax.random.permutation(jax.random.fold_in(own, 1), rows)]
    offset_by = jax.random.randint(jax.random.fold_in(own, 2), (rows, 1), 0, top)
    return jnp.take_along_axis(grid, (jnp.arange(top)[None, :] + offset_by) % top, axis=1)


def shares(number_of, total, limit, skew, full):
    loads = [(1 << 20) // math.isqrt(grade ** skew) + 1 for grade in range(1, number_of + 1)]
    largest = limit if full else min(limit, max(-(-total // number_of), total * loads[0] // sum(loads)))
    least = 1 if total - largest >= number_of - 1 else 0
    counts, spare = [largest] + [least] * (number_of - 1), total - largest - least * (number_of - 1)
    while spare > 0:
        movable = [i for i in range(1, number_of) if counts[i] < largest] or [i for i in range(1, number_of) if counts[i] < limit]
        mass, left = sum([loads[i] for i in movable]), spare
        for i in movable:
            addition = min(limit - counts[i], max(1, left * loads[i] // mass), spare)
            counts[i] = counts[i] + addition
            spare = spare - addition
    return np.array(counts)


def centred(key, dims, deviation, bound, shards=(), held_as=jnp.bfloat16):
    entries = jax.random.normal(key, dims, jnp.float32) * deviation
    if len(shards) > 0:
        entries = shard_levels(key, dims, shards, -0.22, 0.18) * entries
    return jnp.clip(entries, min=-bound, max=bound).astype(held_as)


def setup_inputs(seed: int = 0) -> dict:
    key_of = jax.random.split(jax.random.key(seed), 15)
    hidden = centred(key_of[0], (REQ, NEW_TOK, D), 0.5, 4.0, ((0, 4), (1, 8)))
    queries = draw_queries(jax.random.fold_in(key_of[14], 71), 0)
    fresh_latent = draw_fresh_latent(jax.random.fold_in(key_of[14], 71), 0)
    latent_cache = draw_latent_cache(jax.random.fold_in(key_of[14], 71), 0)
    page_table = jax.vmap(lambda own: jax.random.permutation(own, POOL))(jax.random.split(key_of[4], REQ)).reshape((REQ, POOL)).astype(jnp.int32)
    cache_lengths = draw_cache_lengths(jax.random.fold_in(key_of[14], 71), 0)
    routes_keys = jax.random.split(jax.random.fold_in(key_of[6], 1), REQ * NEW_TOK // TOK_DEV)
    routes_turns = jax.random.permutation(jax.random.fold_in(key_of[6], 3), REQ * NEW_TOK // TOK_DEV)
    routes = jax.vmap(lambda own, number: shared_out(jax.random.fold_in(key_of[6], 2), own, number, TOK_DEV, EXPERTS, TOP, CAP, 2))(routes_keys, routes_turns).reshape((REQ, NEW_TOK, TOP))
    route_gates = jnp.clip(0.05 + 0.39999999 * jax.random.uniform(key_of[7], (REQ, NEW_TOK, TOP), jnp.float32) ** shard_levels(key_of[7], (REQ, NEW_TOK, TOP), ((0, 4), (1, 8)), -0.2, 0.2), 0.05, 0.45)
    kv_up = centred(key_of[8], (LAT, H * (NOPE + VD)), LAT ** -0.5, 0.25)
    out_proj = centred(key_of[9], (H * VD, D), (H * VD) ** -0.5, 0.125)
    latent_gain = jnp.clip(1.0 + 0.18 * jax.random.normal(key_of[10], (LAT,), jnp.float32), 0.1, 1.9)
    norm_gain = jnp.clip(1.0 + 0.18 * jax.random.normal(key_of[11], (D,), jnp.float32), 0.1, 1.9)
    expert_in = centred(key_of[12], (SLABS, D, 2 * HALF), D ** -0.5, 0.125, ((0, 32),))
    expert_out = centred(key_of[13], (SLABS, HALF, D), FF_E ** -0.5, 0.15625, ((0, 32),))
    return dict(hidden=hidden, queries=queries, fresh_latent=fresh_latent, latent_cache=latent_cache, page_table=page_table, cache_lengths=cache_lengths, routes=routes, route_gates=route_gates, kv_up=kv_up, out_proj=out_proj, latent_gain=latent_gain, norm_gain=norm_gain, expert_in=expert_in, expert_out=expert_out)


epsilon = 1e-06
theta_base = 10000.0

def rotary(values, angles):
    half_width = values.shape[-1] // 2
    front_part = values[..., :half_width]
    back_part = values[..., half_width:]
    cosine = jnp.cos(angles)
    sine_part = jnp.sin(angles)
    return jnp.concatenate([front_part * cosine - back_part * sine_part, back_part * cosine + front_part * sine_part], axis=-1)

def rms_scale(values, gain):
    return values * lax.rsqrt(lax.optimization_barrier(jnp.mean(values * values, axis=-1, keepdims=True)) + epsilon) * gain

def reference(hidden, queries, fresh_latent, latent_cache, page_table, cache_lengths, routes, route_gates, kv_up, out_proj, latent_gain, norm_gain, expert_in, expert_out):
    score_scale = 1.0 / math.sqrt(NOPE + ROPE)
    weights = kv_up.astype(jnp.float32).reshape(LAT, H, NOPE + VD)
    frequency = theta_base ** (-jnp.arange(ROPE // 2, dtype=jnp.float32) * 2.0 / ROPE)

    def request_attention(request):
        length = cache_lengths[request]
        positions = length + jnp.arange(NEW_TOK, dtype=jnp.int32)
        angles = positions.astype(jnp.float32)[:, None] * frequency[None, :]
        raw_latent = fresh_latent[request].astype(jnp.float32)
        latent = rms_scale(raw_latent[:, :LAT], latent_gain.astype(jnp.float32)).astype(jnp.bfloat16)
        key_rotated = rotary(raw_latent[:, LAT:], angles).astype(jnp.bfloat16)
        query_rows = queries[request].astype(jnp.float32).reshape(NEW_TOK, H, NOPE + ROPE)
        query_rotated = rotary(query_rows[:, :, NOPE:], angles[:, None, :]).astype(jnp.bfloat16)
        query_latent = jnp.einsum('thn,lhn->thl', query_rows[:, :, :NOPE], weights[:, :, :NOPE]).astype(jnp.bfloat16)
        pages = jnp.take(latent_cache[request], page_table[request], axis=0).reshape(CTX_MAX, LAT + ROPE)
        keys_latent = jnp.concatenate([pages[:, :LAT], latent], axis=0)
        keys_rotated = jnp.concatenate([pages[:, LAT:], key_rotated], axis=0)
        cache_positions = jnp.arange(CTX_MAX, dtype=jnp.int32)
        key_positions = jnp.concatenate([cache_positions, positions])
        key_valid = jnp.concatenate([cache_positions < length, jnp.ones((NEW_TOK,), dtype=bool)])
        allowed = key_valid[None, :] & (key_positions[None, :] <= positions[:, None])

        def one_head(head_index):
            head_query = jnp.take(query_latent, head_index, axis=1)
            head_rotated = jnp.take(query_rotated, head_index, axis=1)
            scores = jnp.dot(head_query, keys_latent.T, preferred_element_type=jnp.float32)
            scores = (scores + jnp.dot(head_rotated, keys_rotated.T, preferred_element_type=jnp.float32)) * score_scale
            scores = jnp.where(allowed, scores, -jnp.inf)
            highest = lax.optimization_barrier(jnp.max(scores, axis=1, keepdims=True))
            soft_weights = jnp.exp(scores - highest)
            totals = lax.optimization_barrier(jnp.sum(soft_weights, axis=1, keepdims=True))
            mixed = jnp.dot(soft_weights.astype(jnp.bfloat16), keys_latent, preferred_element_type=jnp.float32) / totals
            return mixed.astype(jnp.bfloat16)
        mixed_heads = lax.map(one_head, jnp.arange(H))
        head_out = jnp.einsum('htl,lhv->thv', mixed_heads.astype(jnp.float32), weights[:, :, NOPE:]).astype(jnp.bfloat16)
        attended = jnp.dot(head_out.reshape(NEW_TOK, H * VD), out_proj, preferred_element_type=jnp.float32)
        return (attended, jnp.concatenate([latent, key_rotated], axis=1))
    attended_all, new_latent = lax.map(request_attention, jnp.arange(REQ))
    residual = hidden.astype(jnp.float32) + attended_all
    normed = rms_scale(residual, norm_gain.astype(jnp.float32)).astype(jnp.bfloat16).reshape(REQ * NEW_TOK, D)
    flat_routes = routes.reshape(-1)
    flat_gates = route_gates.reshape(-1)
    token_of = jnp.arange(REQ * NEW_TOK * TOP, dtype=jnp.int32) // TOP
    most_rows = N_REQ * N_TOK * CAP

    def expert_step(carry, expert):
        named = flat_routes == expert
        chosen = jnp.nonzero(named, size=most_rows, fill_value=0)[0].astype(jnp.int32)
        live = jnp.arange(most_rows, dtype=jnp.int32) < jnp.sum(named.astype(jnp.int32))
        tokens_here = jnp.take(token_of, chosen)
        selected = jnp.take(normed, tokens_here, axis=0)
        gate_scale = jnp.where(live, jnp.take(flat_gates, chosen), 0.0)
        summed = jnp.zeros((most_rows, D), dtype=jnp.float32)
        for slab_half in range(2):
            slab_index = 2 * expert + slab_half
            projected = jnp.dot(selected, expert_in[slab_index], preferred_element_type=jnp.float32)
            active = (jax.nn.silu(projected[:, :HALF]) * projected[:, HALF:]).astype(jnp.bfloat16)
            slab_result = lax.optimization_barrier(jnp.dot(active, expert_out[slab_index], preferred_element_type=jnp.float32).astype(jnp.bfloat16))
            summed = summed + slab_result.astype(jnp.float32)
        carry = carry.at[tokens_here].add(gate_scale[:, None] * summed)
        return (carry, None)
    routed, unused = lax.scan(expert_step, jnp.zeros((REQ * NEW_TOK, D), dtype=jnp.float32), jnp.arange(EXPERTS, dtype=jnp.int32))
    layer_out = (residual + routed.reshape(REQ, NEW_TOK, D)).astype(jnp.bfloat16)
    return (layer_out, new_latent)
```

```python
import functools
import math

import jax
import jax.numpy as jnp
from jax import lax
from jax.experimental import pallas as pl
from jax.experimental.pallas import tpu as pltpu
from jax.sharding import Mesh
from jax.sharding import PartitionSpec as P

H = 16
NOPE = 128
VD = 128
CAP = 14
PLANES = 4
PAIR = 2
GROUPS = 2
PARTS = 2

epsilon = 1e-06
theta_base = 10000.0
hidden_score = -1e30
PLANE_AXES = ("x", "core", "y")
MIB = 1 << 20
FACT_ROWS = 16
NEAR = [(0, 1), (1, 0), (2, 3), (3, 2)]
MIDDLE = [(1, 2), (2, 1)]
OUTWARD = [(1, 0), (2, 3)]
INWARD = [(0, 1), (3, 2)]


def shifted(values, axis, step):
    count = lax.axis_size(axis)
    return lax.ppermute(values, axis, [(i, (i + step) % count) for i in range(count)])


def entries_kernel(fresh_ref, page_ref, facts_ref, cos_ref, sin_ref, gain_ref, block_ref, new_ref):
    latent_width = gain_ref.shape[0] * gain_ref.shape[1]
    entry_width = fresh_ref.shape[0]
    half = cos_ref.shape[0]
    rows = fresh_ref.shape[1]
    raw = fresh_ref[:latent_width, :].astype(jnp.float32)
    mean = jnp.mean(raw * raw, axis=0, keepdims=True)
    gain = jnp.concatenate(
        [
            jnp.broadcast_to(gain_ref[i : i + 1, :], (rows, gain_ref.shape[1])).T
            for i in range(gain_ref.shape[0])
        ],
        axis=0,
    )
    latent = (raw * lax.rsqrt(mean + epsilon) * gain).astype(jnp.bfloat16)
    front = fresh_ref[latent_width : latent_width + half, :].astype(jnp.float32)
    back = fresh_ref[latent_width + half :, :].astype(jnp.float32)
    cosine = cos_ref[...]
    sine = sin_ref[...]
    turned_front = (front * cosine - back * sine).astype(jnp.bfloat16)
    turned_back = (back * cosine + front * sine).astype(jnp.bfloat16)
    new_ref[:latent_width, :] = latent
    new_ref[latent_width : latent_width + half, :] = turned_front
    new_ref[latent_width + half :, :] = turned_back
    block_ref[:entry_width, :rows] = page_ref[...]
    block_ref[:latent_width, rows:] = latent
    block_ref[latent_width : latent_width + half, rows:] = turned_front
    block_ref[latent_width + half : entry_width, rows:] = turned_back
    block_ref[entry_width:, rows:] = facts_ref[...]
    block_ref[entry_width:, :rows] = facts_ref[...]


def attend(nope_ref, rotated_ref, up_ref, facts_ref, marks_ref, keys_ref, score_scale):
    latent_width = up_ref.shape[0]
    head_width = NOPE + VD
    keys_latent = keys_ref[:latent_width, :]
    keys_rotated = keys_ref[latent_width:, :]
    rows = nope_ref.shape[0]
    first_row = (facts_ref[1] * facts_ref[3] + facts_ref[2]) * rows
    query_rows = lax.broadcasted_iota(jnp.int32, (PAIR * rows, 1), 0)
    allowed = marks_ref[...] <= lax.rem(query_rows, rows) + first_row
    scores = []
    for group in range(GROUPS):
        heads = range(group * PAIR, (group + 1) * PAIR)
        query_latent = jnp.concatenate(
            [
                lax.dot_general(
                    nope_ref[:, i * NOPE : (i + 1) * NOPE],
                    up_ref[:, i * head_width : i * head_width + NOPE],
                    (((1,), (1,)), ((), ())),
                    preferred_element_type=jnp.float32,
                ).astype(jnp.bfloat16)
                for i in heads
            ],
            axis=0,
        )
        query_rotated = jnp.concatenate([rotated_ref[i] for i in heads], axis=0)
        value = jnp.dot(query_latent, keys_latent, preferred_element_type=jnp.float32)
        value = value + jnp.dot(query_rotated, keys_rotated, preferred_element_type=jnp.float32)
        scores.append(jnp.where(allowed, value, hidden_score))
    results = []
    for group in range(GROUPS):
        highest = jnp.max(scores[group], axis=1, keepdims=True)
        soft = jnp.exp((scores[group] - highest) * score_scale)
        totals = jnp.sum(soft, axis=1, keepdims=True)
        mixed = lax.dot_general(
            soft.astype(jnp.bfloat16),
            keys_latent,
            (((1,), (1,)), ((), ())),
            preferred_element_type=jnp.float32,
        )
        results.append((highest, totals, mixed))
    return results


def fill_keys(facts_ref, block_refs, keys_ref, marks_ref, first_slot, y_count, rows):
    width = block_refs[0].shape[1]
    length, z_index, y_index = facts_ref[0], facts_ref[1], facts_ref[2]
    low = z_index < 2
    pool = facts_ref.shape[0] - 4
    page_size = width - rows
    for index, block_ref in enumerate(block_refs):
        keys_ref[:, index * width : (index + 1) * width] = block_ref[: keys_ref.shape[0], :]
        slot = first_slot + index // y_count
        z_source = (
            z_index,
            z_index + 1 - 2 * lax.rem(z_index, 2),
            jnp.where(low, 2, 1),
            jnp.where(low, 3, 0),
        )[slot]
        y_source = lax.rem(y_index + y_count - index % y_count, y_count)
        source = z_source * y_count + y_source
        logical = jnp.int32(0)
        for place in range(pool):
            logical = logical + jnp.where(facts_ref[4 + place] == source, place, 0)
        cached = lax.broadcasted_iota(jnp.int32, (1, page_size), 1) + logical * page_size
        marks_ref[:, index * width : index * width + page_size] = jnp.where(
            cached < length, -1, 1 << 30
        )
        marks_ref[:, index * width + page_size : (index + 1) * width] = (
            lax.broadcasted_iota(jnp.int32, (1, rows), 1) + source * rows
        )


def merged(result, group, old_refs, score_scale):
    highest, totals, mixed = result
    old_highest, old_totals, old_mixed = [ref[group] for ref in old_refs]
    top = jnp.maximum(highest, old_highest)
    fresh = jnp.exp((highest - top) * score_scale)
    fading = jnp.exp((old_highest - top) * score_scale)
    return top, totals * fresh + old_totals * fading, mixed * fresh + old_mixed * fading


def first_attention_kernel(score_scale, first_slot, y_count, block_count, *refs):
    facts_ref, nope_ref, rotated_ref, up_ref = refs[:4]
    block_refs = refs[4 : 4 + block_count]
    *old_refs, highest_ref, totals_ref, mixed_ref, keys_ref, marks_ref = refs[4 + block_count :]

    @pl.when(pl.program_id(0) == 0)
    def _():
        fill_keys(
            facts_ref, block_refs, keys_ref, marks_ref, first_slot, y_count, nope_ref.shape[0]
        )

    results = attend(nope_ref, rotated_ref, up_ref, facts_ref, marks_ref, keys_ref, score_scale)
    for group, result in enumerate(results):
        if old_refs:
            result = merged(result, group, old_refs, score_scale)
        highest, totals, mixed = result
        highest_ref[group] = highest
        totals_ref[group] = totals
        mixed_ref[group] = mixed


def last_attention_kernel(score_scale, first_slot, y_count, block_count, *refs):
    facts_ref, nope_ref, rotated_ref, up_ref = refs[:4]
    block_refs = refs[4 : 4 + block_count]
    old_refs = refs[4 + block_count : 7 + block_count]
    proj_ref, hidden_ref, gain_ref = refs[7 + block_count : 10 + block_count]
    residual_ref, left_ref, right_ref, keys_ref, marks_ref, total_ref = refs[10 + block_count :]
    step = pl.program_id(0)
    rows = hidden_ref.shape[0]
    head_width = NOPE + VD

    @pl.when(step == 0)
    def _():
        fill_keys(facts_ref, block_refs, keys_ref, marks_ref, first_slot, y_count, rows)

    results = attend(nope_ref, rotated_ref, up_ref, facts_ref, marks_ref, keys_ref, score_scale)
    outs = []
    for group, result in enumerate(results):
        _, totals, mixed = merged(result, group, old_refs, score_scale)
        mixed = (mixed / totals).astype(jnp.bfloat16)
        for i in range(PAIR):
            head = group * PAIR + i
            outs.append(
                jnp.dot(
                    mixed[i * rows : (i + 1) * rows],
                    up_ref[:, head * head_width + NOPE : (head + 1) * head_width],
                    preferred_element_type=jnp.float32,
                ).astype(jnp.bfloat16)
            )
    head_out = jnp.concatenate(outs, axis=1)
    part = jnp.dot(head_out, proj_ref[...], preferred_element_type=jnp.float32)

    @pl.when(step == 0)
    def _():
        total_ref[...] = part

    @pl.when(step > 0)
    def _():
        total_ref[...] += part

    @pl.when(step == pl.num_programs(0) - 1)
    def _():
        residual = hidden_ref[...].astype(jnp.float32) + total_ref[...]
        residual_ref[...] = residual
        mean = jnp.mean(residual * residual, axis=1, keepdims=True)
        normed = (residual * lax.rsqrt(mean + epsilon) * gain_ref[...]).astype(jnp.bfloat16)
        left_ref[...] = normed[:, : left_ref.shape[1]]
        right_ref[...] = normed[:, left_ref.shape[1] :]


def attention_call(score_scale, first_slot, y_count, queries, blocks, old, tail):
    facts, nope, rotated, up = queries
    rows = nope.shape[0]
    latent_width = up.shape[0]
    block_height, width = blocks[0].shape
    keys = width * len(blocks)
    rotary_width = rotated.shape[2]
    heads = PAIR * GROUPS
    whole = lambda *shape: pl.BlockSpec(shape, lambda s: (0,) * len(shape))
    state_specs = [
        pl.BlockSpec((GROUPS, PAIR * rows, size), lambda s: (s, 0, 0))
        for size in (1, 1, latent_width)
    ]
    in_specs = [
        pl.BlockSpec(memory_space=pltpu.SMEM),
        pl.BlockSpec((rows, heads * NOPE), lambda s: (0, s)),
        pl.BlockSpec((heads, rows, rotary_width), lambda s: (s, 0, 0)),
        pl.BlockSpec((latent_width, heads * (NOPE + VD)), lambda s: (0, s)),
    ] + [whole(block_height, width)] * len(blocks)
    scratch = [
        pltpu.VMEM((latent_width + rotary_width, keys), jnp.bfloat16),
        pltpu.VMEM((1, keys), jnp.int32),
    ]
    if old:
        in_specs += state_specs
    if tail:
        proj, hidden, gain = tail
        model_width = hidden.shape[1]
        kernel = last_attention_kernel
        in_specs += [
            pl.BlockSpec((heads * VD, model_width), lambda s: (s, 0)),
            whole(rows, model_width),
            whole(1, model_width),
        ]
        out_specs = [whole(rows, model_width)] + [whole(rows, model_width // 2)] * 2
        out_shape = [
            jax.ShapeDtypeStruct((rows, model_width), jnp.float32),
            jax.ShapeDtypeStruct((rows, model_width // 2), jnp.bfloat16),
            jax.ShapeDtypeStruct((rows, model_width // 2), jnp.bfloat16),
        ]
        scratch.append(pltpu.VMEM((rows, model_width), jnp.float32))
    else:
        kernel = first_attention_kernel
        out_specs = state_specs
        out_shape = [
            jax.ShapeDtypeStruct((H // PAIR, PAIR * rows, size), jnp.float32)
            for size in (1, 1, latent_width)
        ]
    return pl.pallas_call(
        functools.partial(kernel, score_scale, first_slot, y_count, len(blocks)),
        grid=(H // heads,),
        in_specs=in_specs,
        out_specs=out_specs,
        out_shape=out_shape,
        scratch_shapes=scratch,
        compiler_params=pltpu.CompilerParams(vmem_limit_bytes=56 * MIB),
        cost_estimate=pl.CostEstimate(
            flops=2 * H * rows * keys * (2 * latent_width + rotary_width),
            bytes_accessed=16 * MIB,
            transcendentals=H * rows * keys,
        ),
    )(facts, nope, rotated, up, *blocks, *old, *tail)


def experts_kernel(slabs_each, sorting, x_ref, *refs):
    if sorting:
        take_ref, put_ref = refs[:2]
        refs = refs[2:]
    in_refs = refs[:PARTS]
    out_weight_refs = refs[PARTS : 2 * PARTS]
    result_ref = refs[2 * PARTS]
    rows_ref, total_ref = refs[2 * PARTS + 1 :]
    expert = pl.program_id(0)
    slab = pl.program_id(1)

    @pl.when(slab == 0)
    def _():
        if sorting:
            rows_ref[...] = jnp.dot(
                take_ref[0], x_ref[...], preferred_element_type=jnp.float32
            ).astype(jnp.bfloat16)
        else:
            rows_ref[...] = x_ref[...]

    depth = in_refs[0].shape[1]
    projected = None
    for index, in_ref in enumerate(in_refs):
        piece = jnp.dot(
            rows_ref[:, index * depth : (index + 1) * depth],
            in_ref[0],
            preferred_element_type=jnp.float32,
        )
        projected = piece if projected is None else projected + piece
    piece_half = out_weight_refs[0].shape[1]
    half = piece_half * PARTS
    active = (jax.nn.silu(projected[:, :half]) * projected[:, half:]).astype(jnp.bfloat16)
    part = None
    for index, out_weight_ref in enumerate(out_weight_refs):
        piece = jnp.dot(
            active[:, index * piece_half : (index + 1) * piece_half],
            out_weight_ref[0],
            preferred_element_type=jnp.float32,
        )
        part = piece if part is None else part + piece

    if slabs_each > 1:

        @pl.when(slab == 0)
        def _():
            total_ref[...] = part

    @pl.when(slab == slabs_each - 1)
    def _():
        value = part
        if slabs_each > 1:
            value = value + total_ref[...]
        value = value.astype(jnp.bfloat16)
        if sorting:
            value = jnp.dot(put_ref[0], value, preferred_element_type=jnp.float32).astype(
                jnp.bfloat16
            )

            @pl.when(expert == 0)
            def _():
                result_ref[...] = value

            @pl.when(expert > 0)
            def _():
                result_ref[...] += value
        else:
            result_ref[...] = value


def experts(x, expert_in, expert_out, experts_here, group):
    rows, width = x.shape
    slabs_each = expert_in.shape[0] // experts_here
    half = expert_out.shape[1]
    each = rows // experts_here
    sorting = experts_here > 1
    operands = [x]
    in_specs = [pl.BlockSpec((rows, width), lambda e, s: (0, 0))]
    if sorting:
        place = jnp.arange(each, dtype=jnp.int32)
        target = (
            (place // group * experts_here)[None, :]
            + jnp.arange(experts_here, dtype=jnp.int32)[:, None]
        ) * group + (place % group)[None, :]
        column = jnp.arange(rows, dtype=jnp.int32)
        take = (target[:, :, None] == column[None, None, :]).astype(jnp.bfloat16)
        put = (target[:, None, :] == column[None, :, None]).astype(jnp.bfloat16)
        operands += [take, put]
        in_specs += [
            pl.BlockSpec((1, each, rows), lambda e, s: (e, 0, 0)),
            pl.BlockSpec((1, rows, each), lambda e, s: (e, 0, 0)),
        ]

    def piece(height, columns, index):
        return pl.BlockSpec((1, height, columns), lambda e, s: (e * slabs_each + s, index, 0))

    operands += [expert_in] * PARTS + [expert_out] * PARTS
    in_specs += [piece(width // PARTS, 2 * half, i) for i in range(PARTS)]
    in_specs += [piece(half // PARTS, width, i) for i in range(PARTS)]
    return pl.pallas_call(
        functools.partial(experts_kernel, slabs_each, sorting),
        grid=(experts_here, slabs_each),
        in_specs=in_specs,
        out_specs=pl.BlockSpec((rows, width), lambda e, s: (0, 0)),
        out_shape=jax.ShapeDtypeStruct((rows, width), jnp.bfloat16),
        scratch_shapes=[
            pltpu.VMEM((each, width), jnp.bfloat16),
            pltpu.VMEM((each, width), jnp.float32),
        ],
        compiler_params=pltpu.CompilerParams(vmem_limit_bytes=58 * MIB),
        cost_estimate=pl.CostEstimate(
            flops=6 * rows * width * half * slabs_each,
            bytes_accessed=2 * 3 * width * half * experts_here * slabs_each,
            transcendentals=rows * half,
        ),
    )(*operands)


def pack_kernel(layers, place_ref, *refs):
    *token_refs, result_ref = refs
    sides = len(token_refs) // (2 * layers)
    width = token_refs[0].shape[1]
    for side in range(sides):
        blocks = []
        for block in range(2):
            value = None
            for layer in range(layers):
                piece = token_refs[(block * layers + layer) * sides + side][...]
                value = piece if value is None else value + piece
            blocks.append(value)
        tokens = jnp.concatenate(blocks, axis=0)
        result_ref[:, side * width : (side + 1) * width] = jnp.dot(
            place_ref[...], tokens, preferred_element_type=jnp.float32
        ).astype(jnp.bfloat16)


def pack(placing, blocks):
    layers = len(blocks[0])
    operands = [half for block in blocks for layer in block for half in layer]
    rows, tokens = placing.shape
    width = sum(half.shape[1] for half in blocks[0][0])
    return pl.pallas_call(
        functools.partial(pack_kernel, layers),
        out_shape=jax.ShapeDtypeStruct((rows, width), jnp.bfloat16),
        compiler_params=pltpu.CompilerParams(vmem_limit_bytes=40 * MIB),
        cost_estimate=pl.CostEstimate(
            flops=2 * rows * tokens * width, bytes_accessed=6 * rows * width, transcendentals=0
        ),
    )(placing, *operands)


def combine_kernel(weights_ref, rows_ref, *out_refs):
    value = jnp.dot(weights_ref[...], rows_ref[...], preferred_element_type=jnp.float32)
    row = 0
    column = 0
    for out_ref in out_refs:
        height, width = out_ref.shape
        out_ref[...] = value[row : row + height, column : column + width].astype(out_ref.dtype)
        column += width
        if column == value.shape[1]:
            row, column = row + height, 0


def combine(weights, rows, out_shape):
    return pl.pallas_call(
        combine_kernel,
        out_shape=out_shape,
        compiler_params=pltpu.CompilerParams(vmem_limit_bytes=40 * MIB),
        cost_estimate=pl.CostEstimate(
            flops=2 * weights.shape[0] * rows.size,
            bytes_accessed=4 * rows.size,
            transcendentals=0,
        ),
    )(weights, rows)


def finish_kernel(residual_ref, own_ref, *refs):
    *part_refs, out_ref = refs
    width = part_refs[0].shape[1]
    for side in range(2):
        columns = slice(side * width, (side + 1) * width)
        value = residual_ref[:, columns] + own_ref[:, columns]
        for part_ref in part_refs[side::2]:
            value = value + part_ref[...].astype(jnp.float32)
        out_ref[:, columns] = value.astype(out_ref.dtype)


def local(
    hidden,
    queries,
    fresh_latent,
    latent_cache,
    page_table,
    cache_lengths,
    routes,
    route_gates,
    kv_up,
    out_proj,
    latent_gain,
    norm_gain,
    expert_in,
    expert_out,
):
    row_count = hidden.shape[1]
    model_width = hidden.shape[2]
    latent_width = latent_gain.shape[0]
    entry_width = fresh_latent.shape[2]
    rotary_width = entry_width - latent_width
    half_rotary = rotary_width // 2
    score_scale = 1.0 / math.sqrt(NOPE + rotary_width)
    length = cache_lengths[0]
    y_count = lax.axis_size("y")
    z_index = lax.axis_index("z")
    y_index = lax.axis_index("y")
    tok_index = z_index * y_count + y_index
    tok_count = PLANES * y_count

    first_row = tok_index * row_count
    offsets = jnp.arange(row_count, dtype=jnp.int32)
    positions = (length + first_row + offsets).astype(jnp.float32)
    frequency = theta_base ** (-jnp.arange(half_rotary, dtype=jnp.float32) * 2.0 / rotary_width)
    angles = frequency[:, None] * positions[None, :]
    cosine = jnp.cos(angles)
    sine = jnp.sin(angles)
    page_size = latent_cache.shape[2]
    top_count = routes.shape[2]
    own_facts = jnp.concatenate([routes[0].astype(jnp.bfloat16), route_gates[0].astype(jnp.bfloat16)], axis=1).T
    own_facts = jnp.pad(own_facts, ((0, FACT_ROWS - 2 * top_count), (0, 0)))
    own_block, new_entries = pl.pallas_call(
        entries_kernel,
        out_shape=[
            jax.ShapeDtypeStruct((entry_width + FACT_ROWS, page_size + row_count), jnp.bfloat16),
            jax.ShapeDtypeStruct((entry_width, row_count), jnp.bfloat16),
        ],
    )(
        fresh_latent[0].T,
        latent_cache[0, 0].T,
        own_facts,
        cosine,
        sine,
        latent_gain.reshape(latent_width // row_count, row_count),
    )

    inner = jnp.logical_or(z_index == 1, z_index == 2)

    def along_z(values):
        near = lax.ppermute(values, "z", NEAR)
        middle = lax.ppermute(values, "z", MIDDLE)
        middle_far = lax.ppermute(near, "z", MIDDLE)
        outward = lax.ppermute(middle, "z", OUTWARD)
        outward_far = lax.ppermute(middle_far, "z", OUTWARD)
        return near, (middle, outward), (middle_far, outward_far)

    near_block, *far_blocks = along_z(own_block)
    z_blocks = [own_block, near_block] + [jnp.where(inner, *pair) for pair in far_blocks]
    blocks = [
        z_block if j == 0 else shifted(z_block, "y", j)
        for z_block in z_blocks
        for j in range(y_count)
    ]

    query_rows = queries[0].reshape(row_count, H, NOPE + rotary_width)
    nope = query_rows[:, :, :NOPE].reshape(row_count, H * NOPE)
    turning = query_rows[:, :, NOPE:].astype(jnp.float32).transpose(1, 0, 2)
    front, back = turning[:, :, :half_rotary], turning[:, :, half_rotary:]
    token_cosine, token_sine = cosine.T[None], sine.T[None]
    rotated = jnp.concatenate(
        [front * token_cosine - back * token_sine, back * token_cosine + front * token_sine],
        axis=2,
    ).astype(jnp.bfloat16)

    places = jnp.stack(
        [length, z_index.astype(jnp.int32), y_index.astype(jnp.int32), jnp.int32(y_count)]
    )
    prepared = (jnp.concatenate([places, page_table[0]]), nope, rotated, kv_up)
    own_blocks, middle_blocks, last_blocks = (
        blocks[: 2 * y_count],
        blocks[2 * y_count : 3 * y_count],
        blocks[3 * y_count :],
    )
    state = attention_call(score_scale, 0, y_count, prepared, own_blocks, (), ())
    middle_blocks, last_blocks[0] = lax.optimization_barrier((middle_blocks, last_blocks[0]))
    state = attention_call(score_scale, 2, y_count, prepared, middle_blocks, state, ())
    column_facts = [block[entry_width:, page_size:] for block in z_blocks]
    column_facts, state = lax.optimization_barrier((column_facts, state))
    residual, *normed = attention_call(
        score_scale,
        3,
        y_count,
        prepared,
        last_blocks,
        state,
        (out_proj, hidden[0], norm_gain[None, :]),
    )

    slabs_here = expert_in.shape[0]
    experts_here = max(1, slabs_here // 2)
    x_count = lax.axis_size("x")
    plane_devices = x_count * 2 * y_count
    place = jnp.arange(plane_devices, dtype=jnp.int32)
    device_index = (place // y_count) * tok_count + z_index * y_count + place % y_count
    expert_ids = (
        (device_index * slabs_here)[:, None] // 2 + jnp.arange(experts_here, dtype=jnp.int32)
    ).reshape(-1)
    expert_ids = expert_ids.astype(jnp.float32)
    earlier = (offsets[:, None] < offsets[None, :]).astype(jnp.bfloat16)
    group = 2 * CAP
    expert_places = plane_devices * experts_here
    row_ids = jnp.arange(expert_places * group, dtype=jnp.int32)
    spread = (
        row_ids[:, None] // group == jnp.arange(expert_places, dtype=jnp.int32)[None, :]
    ).astype(jnp.bfloat16)
    wanted = (row_ids % group).astype(jnp.float32)[:, None]

    def pair_matrices(first, second):
        codes = []
        weights = []
        for index, fact in enumerate((first, second)):
            match = fact[None, :top_count, :].astype(jnp.float32) == expert_ids[:, None, None]
            named = jnp.any(match, axis=1)
            gates = fact[None, top_count : 2 * top_count, :].astype(jnp.float32)
            weights.append(jnp.sum(jnp.where(match, gates, 0.0), axis=1))
            rank = jnp.dot(
                named.astype(jnp.bfloat16), earlier, preferred_element_type=jnp.float32
            )
            codes.append(jnp.where(named, rank + index * CAP, -1.0))
        code = jnp.concatenate(codes, axis=1).astype(jnp.bfloat16)
        weight = jnp.concatenate(weights, axis=1).astype(jnp.bfloat16)
        chosen = jnp.dot(spread, code, preferred_element_type=jnp.float32) == wanted
        gate_rows = jnp.dot(spread, weight, preferred_element_type=jnp.float32)
        gate_rows = jnp.where(chosen, gate_rows, 0.0).astype(jnp.bfloat16)
        return chosen.astype(jnp.bfloat16), gate_rows.T

    near_matrices = pair_matrices(column_facts[0], column_facts[1])
    far_matrices = pair_matrices(column_facts[2], column_facts[3])

    def exchanged(values):
        return lax.all_to_all(values, PLANE_AXES, split_axis=0, concat_axis=0, tiled=True)

    def all_exchanged(rows):
        rows = rows.reshape(plane_devices, experts_here * group, model_width)
        return exchanged(rows).reshape(expert_places * group, model_width)

    near, *far = zip(*[along_z(half) for half in normed])
    near, middle = lax.optimization_barrier((near, [layers[0] for layers in far[0]]))
    far[0] = [(value, layers[1]) for value, layers in zip(middle, far[0])]
    near_rows = all_exchanged(pack(near_matrices[0], [[normed], [near]]))
    far = [list(zip(*block)) for block in far]
    near_rows, far = lax.optimization_barrier((near_rows, far))
    far_rows = all_exchanged(pack(far_matrices[0], far))
    near_rows = experts(near_rows, expert_in, expert_out, experts_here, group)
    far_rows = experts(far_rows, expert_in, expert_out, experts_here, group)

    def added(first, second):
        value = first.astype(jnp.float32) + second.astype(jnp.float32)
        return value.astype(jnp.bfloat16)

    def moved(value, pairs):
        return lax.ppermute(value, "z", pairs)

    half_shape = jax.ShapeDtypeStruct((row_count, model_width // 2), jnp.bfloat16)
    whole_shape = jax.ShapeDtypeStruct((row_count, model_width), jnp.float32)
    returned = combine(far_matrices[1], all_exchanged(far_rows), [half_shape] * 4)
    returned, near_rows = lax.optimization_barrier((returned, near_rows))
    middle_parts, far_parts = returned[:2], returned[2:]
    far_arrived = [moved(part, INWARD) for part in far_parts]
    middle_parts, far_arrived[1] = lax.optimization_barrier((middle_parts, far_arrived[1]))
    far_parts = [moved(added(*pair), MIDDLE) for pair in zip(far_parts, far_arrived)]
    middle_arrived = [moved(part, INWARD) for part in middle_parts]
    own_part, *near_parts = combine(
        near_matrices[1], all_exchanged(near_rows), [whole_shape] + [half_shape] * 2
    )
    own_part, middle_parts, middle_arrived = lax.optimization_barrier(
        (own_part, middle_parts, middle_arrived)
    )
    middle_arrived = [moved(added(*pair), MIDDLE) for pair in zip(middle_parts, middle_arrived)]
    near_arrived = [moved(added(*pair), NEAR) for pair in zip(near_parts, far_parts)]
    layer_out = pl.pallas_call(
        finish_kernel,
        out_shape=jax.ShapeDtypeStruct((row_count, model_width), jnp.bfloat16),
        compiler_params=pltpu.CompilerParams(vmem_limit_bytes=40 * MIB),
    )(residual, own_part, *near_arrived, *middle_arrived)
    return (layer_out[None], new_entries.T[None])


def solution(mesh):
    req_count, tok_count = mesh.devices.shape
    devices = mesh.devices.reshape(req_count // 2, 2, PLANES, tok_count // PLANES)
    fine = Mesh(devices, ("x", "core", "z", "y"))
    req = ("x", "core")
    tok = ("z", "y")
    placed = (
        P(req, tok, None),
        P(req, tok, None),
        P(req, tok, None),
        P(req, tok, None, None),
        P(req, None),
        P(req),
        P(req, tok, None),
        P(req, tok, None),
        P(),
        P(),
        P(),
        P(),
        P(("x", "core", "z", "y"), None, None),
        P(("x", "core", "z", "y"), None, None),
    )
    return jax.shard_map(
        local,
        mesh=fine,
        in_specs=placed,
        out_specs=(P(req, tok, None), P(req, tok, None)),
        check_vma=False,
    )
```

```python
import functools
import math

import jax
import jax.numpy as jnp
from jax import lax
from jax.experimental import pallas as pl
from jax.experimental.pallas import tpu as pltpu
from jax.sharding import Mesh
from jax.sharding import PartitionSpec as P

H = 16
NOPE = 128
VD = 128
CAP = 14
PLANES = 4
PAIR = 2
GROUPS = 2
PARTS = 2

epsilon = 1e-06
theta_base = 10000.0
hidden_score = -1e30
PLANE_AXES = ("x", "core", "y")
MIB = 1 << 20
FACT_ROWS = 16
NEAR = [(0, 1), (1, 0), (2, 3), (3, 2)]
MIDDLE = [(1, 2), (2, 1)]
OUTWARD = [(1, 0), (2, 3)]
ACROSS = [(0, 3), (3, 0)]
FROM_END = [(3, 1), (0, 2)]
TO_END = [(1, 3), (2, 0)]
INWARD = [(0, 1), (3, 2)]


def shifted(values, axis, step):
    count = lax.axis_size(axis)
    return lax.ppermute(values, axis, [(i, (i + step) % count) for i in range(count)])


def entries_kernel(fresh_ref, page_ref, facts_ref, cos_ref, sin_ref, gain_ref, block_ref, new_ref):
    latent_width = gain_ref.shape[0] * gain_ref.shape[1]
    entry_width = fresh_ref.shape[0]
    half = cos_ref.shape[0]
    rows = fresh_ref.shape[1]
    raw = fresh_ref[:latent_width, :].astype(jnp.float32)
    mean = jnp.mean(raw * raw, axis=0, keepdims=True)
    gain = jnp.concatenate(
        [
            jnp.broadcast_to(gain_ref[i : i + 1, :], (rows, gain_ref.shape[1])).T
            for i in range(gain_ref.shape[0])
        ],
        axis=0,
    )
    latent = (raw * lax.rsqrt(mean + epsilon) * gain).astype(jnp.bfloat16)
    front = fresh_ref[latent_width : latent_width + half, :].astype(jnp.float32)
    back = fresh_ref[latent_width + half :, :].astype(jnp.float32)
    cosine = cos_ref[...]
    sine = sin_ref[...]
    turned_front = (front * cosine - back * sine).astype(jnp.bfloat16)
    turned_back = (back * cosine + front * sine).astype(jnp.bfloat16)
    new_ref[:latent_width, :] = latent
    new_ref[latent_width : latent_width + half, :] = turned_front
    new_ref[latent_width + half :, :] = turned_back
    block_ref[:entry_width, :rows] = page_ref[...]
    block_ref[:latent_width, rows:] = latent
    block_ref[latent_width : latent_width + half, rows:] = turned_front
    block_ref[latent_width + half : entry_width, rows:] = turned_back
    block_ref[entry_width:, rows:] = facts_ref[...]
    block_ref[entry_width:, :rows] = facts_ref[...]


def attend(nope_ref, rotated_ref, up_ref, facts_ref, marks_ref, keys_ref, score_scale):
    latent_width = up_ref.shape[0]
    head_width = NOPE + VD
    keys_latent = keys_ref[:latent_width, :]
    keys_rotated = keys_ref[latent_width:, :]
    rows = nope_ref.shape[0]
    first_row = (facts_ref[1] * facts_ref[3] + facts_ref[2]) * rows
    query_rows = lax.broadcasted_iota(jnp.int32, (PAIR * rows, 1), 0)
    allowed = marks_ref[...] <= lax.rem(query_rows, rows) + first_row
    scores = []
    for group in range(GROUPS):
        heads = range(group * PAIR, (group + 1) * PAIR)
        query_latent = jnp.concatenate(
            [
                lax.dot_general(
                    nope_ref[:, i * NOPE : (i + 1) * NOPE],
                    up_ref[:, i * head_width : i * head_width + NOPE],
                    (((1,), (1,)), ((), ())),
                    preferred_element_type=jnp.float32,
                ).astype(jnp.bfloat16)
                for i in heads
            ],
            axis=0,
        )
        query_rotated = jnp.concatenate([rotated_ref[i] for i in heads], axis=0)
        value = jnp.dot(query_latent, keys_latent, preferred_element_type=jnp.float32)
        value = value + jnp.dot(query_rotated, keys_rotated, preferred_element_type=jnp.float32)
        scores.append(jnp.where(allowed, value, hidden_score))
    results = []
    for group in range(GROUPS):
        highest = jnp.max(scores[group], axis=1, keepdims=True)
        soft = jnp.exp((scores[group] - highest) * score_scale)
        totals = jnp.sum(soft, axis=1, keepdims=True)
        mixed = lax.dot_general(
            soft.astype(jnp.bfloat16),
            keys_latent,
            (((1,), (1,)), ((), ())),
            preferred_element_type=jnp.float32,
        )
        results.append((highest, totals, mixed))
    return results


def fill_keys(facts_ref, block_refs, keys_ref, marks_ref, first_slot, y_count, rows):
    width = block_refs[0].shape[1]
    length, z_index, y_index = facts_ref[0], facts_ref[1], facts_ref[2]
    low = z_index < 2
    pool = facts_ref.shape[0] - 4
    page_size = width - rows
    for index, block_ref in enumerate(block_refs):
        keys_ref[:, index * width : (index + 1) * width] = block_ref[: keys_ref.shape[0], :]
        slot = first_slot + index // y_count
        z_source = (
            z_index,
            z_index + 1 - 2 * lax.rem(z_index, 2),
            jnp.where(low, 2, 1),
            jnp.where(low, 3, 0),
        )[slot]
        y_source = lax.rem(y_index + y_count - index % y_count, y_count)
        source = z_source * y_count + y_source
        logical = jnp.int32(0)
        for place in range(pool):
            logical = logical + jnp.where(facts_ref[4 + place] == source, place, 0)
        cached = lax.broadcasted_iota(jnp.int32, (1, page_size), 1) + logical * page_size
        marks_ref[:, index * width : index * width + page_size] = jnp.where(
            cached < length, -1, 1 << 30
        )
        marks_ref[:, index * width + page_size : (index + 1) * width] = (
            lax.broadcasted_iota(jnp.int32, (1, rows), 1) + source * rows
        )


def merged(result, group, old_refs, score_scale):
    highest, totals, mixed = result
    old_highest, old_totals, old_mixed = [ref[group] for ref in old_refs]
    top = jnp.maximum(highest, old_highest)
    fresh = jnp.exp((highest - top) * score_scale)
    fading = jnp.exp((old_highest - top) * score_scale)
    return top, totals * fresh + old_totals * fading, mixed * fresh + old_mixed * fading


def first_attention_kernel(score_scale, first_slot, y_count, block_count, *refs):
    facts_ref, nope_ref, rotated_ref, up_ref = refs[:4]
    block_refs = refs[4 : 4 + block_count]
    highest_ref, totals_ref, mixed_ref, keys_ref, marks_ref = refs[-5:]

    @pl.when(pl.program_id(0) == 0)
    def _():
        fill_keys(
            facts_ref, block_refs, keys_ref, marks_ref, first_slot, y_count, nope_ref.shape[0]
        )

    results = attend(nope_ref, rotated_ref, up_ref, facts_ref, marks_ref, keys_ref, score_scale)
    for group, (highest, totals, mixed) in enumerate(results):
        highest_ref[group] = highest
        totals_ref[group] = totals
        mixed_ref[group] = mixed


def last_attention_kernel(score_scale, first_slot, y_count, block_count, *refs):
    facts_ref, nope_ref, rotated_ref, up_ref = refs[:4]
    block_refs = refs[4 : 4 + block_count]
    old_refs = refs[4 + block_count : 7 + block_count]
    proj_ref, hidden_ref, gain_ref = refs[7 + block_count : 10 + block_count]
    residual_ref, left_ref, right_ref, keys_ref, marks_ref, total_ref = refs[10 + block_count :]
    step = pl.program_id(0)
    rows = hidden_ref.shape[0]
    head_width = NOPE + VD

    @pl.when(step == 0)
    def _():
        fill_keys(facts_ref, block_refs, keys_ref, marks_ref, first_slot, y_count, rows)

    results = attend(nope_ref, rotated_ref, up_ref, facts_ref, marks_ref, keys_ref, score_scale)
    outs = []
    for group, result in enumerate(results):
        _, totals, mixed = merged(result, group, old_refs, score_scale)
        mixed = (mixed / totals).astype(jnp.bfloat16)
        for i in range(PAIR):
            head = group * PAIR + i
            outs.append(
                jnp.dot(
                    mixed[i * rows : (i + 1) * rows],
                    up_ref[:, head * head_width + NOPE : (head + 1) * head_width],
                    preferred_element_type=jnp.float32,
                ).astype(jnp.bfloat16)
            )
    head_out = jnp.concatenate(outs, axis=1)
    part = jnp.dot(head_out, proj_ref[...], preferred_element_type=jnp.float32)

    @pl.when(step == 0)
    def _():
        total_ref[...] = part

    @pl.when(step > 0)
    def _():
        total_ref[...] += part

    @pl.when(step == pl.num_programs(0) - 1)
    def _():
        residual = hidden_ref[...].astype(jnp.float32) + total_ref[...]
        residual_ref[...] = residual
        mean = jnp.mean(residual * residual, axis=1, keepdims=True)
        normed = (residual * lax.rsqrt(mean + epsilon) * gain_ref[...]).astype(jnp.bfloat16)
        left_ref[...] = normed[:, : left_ref.shape[1]]
        right_ref[...] = normed[:, left_ref.shape[1] :]


def attention_call(score_scale, first_slot, y_count, queries, blocks, old, tail, part=None):
    facts, nope, rotated, up = queries
    rows = nope.shape[0]
    latent_width = up.shape[0]
    block_height, width = blocks[0].shape
    keys = width * len(blocks)
    rotary_width = rotated.shape[2]
    heads = PAIR * GROUPS
    whole = lambda *shape: pl.BlockSpec(shape, lambda s: (0,) * len(shape))
    index, count = part or (0, 1)
    steps = H // heads // count
    start = index * steps
    state_specs = [
        pl.BlockSpec((GROUPS, PAIR * rows, size), lambda s: (s + start, 0, 0))
        for size in (1, 1, latent_width)
    ]
    in_specs = [
        pl.BlockSpec(memory_space=pltpu.SMEM),
        pl.BlockSpec((rows, heads * NOPE), lambda s: (0, s + start)),
        pl.BlockSpec((heads, rows, rotary_width), lambda s: (s + start, 0, 0)),
        pl.BlockSpec((latent_width, heads * (NOPE + VD)), lambda s: (0, s + start)),
    ] + [whole(block_height, width)] * len(blocks)
    scratch = [
        pltpu.VMEM((latent_width + rotary_width, keys), jnp.bfloat16),
        pltpu.VMEM((1, keys), jnp.int32),
    ]
    aliases = {}
    if old and part:
        aliases = {len(in_specs) + i: i for i in range(len(old))}
        in_specs += [pl.BlockSpec(memory_space=pl.ANY)] * len(old)
    elif old:
        in_specs += state_specs
    if tail:
        proj, hidden, gain = tail
        model_width = hidden.shape[1]
        kernel = last_attention_kernel
        in_specs += [
            pl.BlockSpec((heads * VD, model_width), lambda s: (s, 0)),
            whole(rows, model_width),
            whole(1, model_width),
        ]
        out_specs = [whole(rows, model_width)] + [whole(rows, model_width // 2)] * 2
        out_shape = [
            jax.ShapeDtypeStruct((rows, model_width), jnp.float32),
            jax.ShapeDtypeStruct((rows, model_width // 2), jnp.bfloat16),
            jax.ShapeDtypeStruct((rows, model_width // 2), jnp.bfloat16),
        ]
        scratch.append(pltpu.VMEM((rows, model_width), jnp.float32))
    else:
        kernel = first_attention_kernel
        out_specs = state_specs
        out_shape = [
            jax.ShapeDtypeStruct((H // PAIR, PAIR * rows, size), jnp.float32)
            for size in (1, 1, latent_width)
        ]
    return pl.pallas_call(
        functools.partial(kernel, score_scale, first_slot, y_count, len(blocks)),
        grid=(steps,),
        in_specs=in_specs,
        out_specs=out_specs,
        out_shape=out_shape,
        scratch_shapes=scratch,
        input_output_aliases=aliases,
        compiler_params=pltpu.CompilerParams(vmem_limit_bytes=56 * MIB),
        cost_estimate=pl.CostEstimate(
            flops=2 * H * rows * keys * (2 * latent_width + rotary_width) // count,
            bytes_accessed=16 * MIB // count,
            transcendentals=H * rows * keys // count,
        ),
    )(facts, nope, rotated, up, *blocks, *old, *tail)


def experts_kernel(slabs_each, sorting, x_ref, *refs):
    if sorting:
        take_ref, put_ref = refs[:2]
        refs = refs[2:]
    in_refs = refs[:PARTS]
    out_weight_refs = refs[PARTS : 2 * PARTS]
    result_ref = refs[2 * PARTS]
    rows_ref, total_ref = refs[2 * PARTS + 1 :]
    expert = pl.program_id(0)
    slab = pl.program_id(1)

    @pl.when(slab == 0)
    def _():
        if sorting:
            rows_ref[...] = jnp.dot(
                take_ref[0], x_ref[...], preferred_element_type=jnp.float32
            ).astype(jnp.bfloat16)
        else:
            rows_ref[...] = x_ref[...]

    depth = in_refs[0].shape[1]
    projected = None
    for index, in_ref in enumerate(in_refs):
        piece = jnp.dot(
            rows_ref[:, index * depth : (index + 1) * depth],
            in_ref[0],
            preferred_element_type=jnp.float32,
        )
        projected = piece if projected is None else projected + piece
    piece_half = out_weight_refs[0].shape[1]
    half = piece_half * PARTS
    active = (jax.nn.silu(projected[:, :half]) * projected[:, half:]).astype(jnp.bfloat16)
    part = None
    for index, out_weight_ref in enumerate(out_weight_refs):
        piece = jnp.dot(
            active[:, index * piece_half : (index + 1) * piece_half],
            out_weight_ref[0],
            preferred_element_type=jnp.float32,
        )
        part = piece if part is None else part + piece

    if slabs_each > 1:

        @pl.when(slab == 0)
        def _():
            total_ref[...] = part

    @pl.when(slab == slabs_each - 1)
    def _():
        value = part
        if slabs_each > 1:
            value = value + total_ref[...]
        value = value.astype(jnp.bfloat16)
        if sorting:
            value = jnp.dot(put_ref[0], value, preferred_element_type=jnp.float32).astype(
                jnp.bfloat16
            )

            @pl.when(expert == 0)
            def _():
                result_ref[...] = value

            @pl.when(expert > 0)
            def _():
                result_ref[...] += value
        else:
            result_ref[...] = value


def experts(x, expert_in, expert_out, experts_here, group):
    rows, width = x.shape
    slabs_each = expert_in.shape[0] // experts_here
    half = expert_out.shape[1]
    each = rows // experts_here
    sorting = experts_here > 1
    operands = [x]
    in_specs = [pl.BlockSpec((rows, width), lambda e, s: (0, 0))]
    if sorting:
        place = jnp.arange(each, dtype=jnp.int32)
        target = (
            (place // group * experts_here)[None, :]
            + jnp.arange(experts_here, dtype=jnp.int32)[:, None]
        ) * group + (place % group)[None, :]
        column = jnp.arange(rows, dtype=jnp.int32)
        take = (target[:, :, None] == column[None, None, :]).astype(jnp.bfloat16)
        put = (target[:, None, :] == column[None, :, None]).astype(jnp.bfloat16)
        operands += [take, put]
        in_specs += [
            pl.BlockSpec((1, each, rows), lambda e, s: (e, 0, 0)),
            pl.BlockSpec((1, rows, each), lambda e, s: (e, 0, 0)),
        ]

    def piece(height, columns, index):
        return pl.BlockSpec((1, height, columns), lambda e, s: (e * slabs_each + s, index, 0))

    operands += [expert_in] * PARTS + [expert_out] * PARTS
    in_specs += [piece(width // PARTS, 2 * half, i) for i in range(PARTS)]
    in_specs += [piece(half // PARTS, width, i) for i in range(PARTS)]
    return pl.pallas_call(
        functools.partial(experts_kernel, slabs_each, sorting),
        grid=(experts_here, slabs_each),
        in_specs=in_specs,
        out_specs=pl.BlockSpec((rows, width), lambda e, s: (0, 0)),
        out_shape=jax.ShapeDtypeStruct((rows, width), jnp.bfloat16),
        scratch_shapes=[
            pltpu.VMEM((each, width), jnp.bfloat16),
            pltpu.VMEM((each, width), jnp.float32),
        ],
        compiler_params=pltpu.CompilerParams(vmem_limit_bytes=58 * MIB),
        cost_estimate=pl.CostEstimate(
            flops=6 * rows * width * half * slabs_each,
            bytes_accessed=2 * 3 * width * half * experts_here * slabs_each,
            transcendentals=rows * half,
        ),
    )(*operands)


def pack_kernel(layers, place_ref, *refs):
    *token_refs, result_ref = refs
    sides = len(token_refs) // (2 * layers)
    width = token_refs[0].shape[1]
    for side in range(sides):
        blocks = []
        for block in range(2):
            value = None
            for layer in range(layers):
                piece = token_refs[(block * layers + layer) * sides + side][...]
                value = piece if value is None else value + piece
            blocks.append(value)
        tokens = jnp.concatenate(blocks, axis=0)
        result_ref[:, side * width : (side + 1) * width] = jnp.dot(
            place_ref[...], tokens, preferred_element_type=jnp.float32
        ).astype(jnp.bfloat16)


def pack(placing, blocks):
    layers = len(blocks[0])
    operands = [half for block in blocks for layer in block for half in layer]
    rows, tokens = placing.shape
    width = sum(half.shape[1] for half in blocks[0][0])
    return pl.pallas_call(
        functools.partial(pack_kernel, layers),
        out_shape=jax.ShapeDtypeStruct((rows, width), jnp.bfloat16),
        compiler_params=pltpu.CompilerParams(vmem_limit_bytes=40 * MIB),
        cost_estimate=pl.CostEstimate(
            flops=2 * rows * tokens * width, bytes_accessed=6 * rows * width, transcendentals=0
        ),
    )(placing, *operands)


def combine_kernel(weights_ref, rows_ref, *out_refs):
    value = jnp.dot(weights_ref[...], rows_ref[...], preferred_element_type=jnp.float32)
    row = 0
    column = 0
    for out_ref in out_refs:
        height, width = out_ref.shape
        out_ref[...] = value[row : row + height, column : column + width].astype(out_ref.dtype)
        column += width
        if column == value.shape[1]:
            row, column = row + height, 0


def combine(weights, rows, out_shape):
    return pl.pallas_call(
        combine_kernel,
        out_shape=out_shape,
        compiler_params=pltpu.CompilerParams(vmem_limit_bytes=40 * MIB),
        cost_estimate=pl.CostEstimate(
            flops=2 * weights.shape[0] * rows.size,
            bytes_accessed=4 * rows.size,
            transcendentals=0,
        ),
    )(weights, rows)


def finish_kernel(residual_ref, own_ref, *refs):
    *part_refs, out_ref = refs
    halves, wholes = part_refs[:2], part_refs[2:]
    width = halves[0].shape[1]
    for side in range(2):
        columns = slice(side * width, (side + 1) * width)
        value = residual_ref[:, columns] + own_ref[:, columns]
        value = value + halves[side][...].astype(jnp.float32)
        for part_ref in wholes:
            value = value + part_ref[:, columns].astype(jnp.float32)
        out_ref[:, columns] = value.astype(out_ref.dtype)


def local(
    hidden,
    queries,
    fresh_latent,
    latent_cache,
    page_table,
    cache_lengths,
    routes,
    route_gates,
    kv_up,
    out_proj,
    latent_gain,
    norm_gain,
    expert_in,
    expert_out,
):
    row_count = hidden.shape[1]
    model_width = hidden.shape[2]
    latent_width = latent_gain.shape[0]
    entry_width = fresh_latent.shape[2]
    rotary_width = entry_width - latent_width
    half_rotary = rotary_width // 2
    score_scale = 1.0 / math.sqrt(NOPE + rotary_width)
    length = cache_lengths[0]
    y_count = lax.axis_size("y")
    z_index = lax.axis_index("z")
    y_index = lax.axis_index("y")
    tok_index = z_index * y_count + y_index
    tok_count = PLANES * y_count

    first_row = tok_index * row_count
    offsets = jnp.arange(row_count, dtype=jnp.int32)
    positions = (length + first_row + offsets).astype(jnp.float32)
    frequency = theta_base ** (-jnp.arange(half_rotary, dtype=jnp.float32) * 2.0 / rotary_width)
    angles = frequency[:, None] * positions[None, :]
    cosine = jnp.cos(angles)
    sine = jnp.sin(angles)
    page_size = latent_cache.shape[2]
    top_count = routes.shape[2]
    own_facts = jnp.concatenate(
        [
            routes[0].T.astype(jnp.bfloat16),
            route_gates[0].T.astype(jnp.bfloat16),
            jnp.zeros((FACT_ROWS - 2 * top_count, row_count), jnp.bfloat16),
        ],
        axis=0,
    )
    own_block, new_entries = pl.pallas_call(
        entries_kernel,
        out_shape=[
            jax.ShapeDtypeStruct((entry_width + FACT_ROWS, page_size + row_count), jnp.bfloat16),
            jax.ShapeDtypeStruct((entry_width, row_count), jnp.bfloat16),
        ],
    )(
        fresh_latent[0].T,
        latent_cache[0, 0].T,
        own_facts,
        cosine,
        sine,
        latent_gain.reshape(latent_width // row_count, row_count),
    )

    inner = jnp.logical_or(z_index == 1, z_index == 2)

    def along_z(values):
        near = lax.ppermute(values, "z", NEAR)
        middle = lax.ppermute(values, "z", MIDDLE)
        middle_far = lax.ppermute(near, "z", MIDDLE)
        outward = lax.ppermute(middle, "z", OUTWARD)
        outward_far = lax.ppermute(middle_far, "z", OUTWARD)
        return near, (middle, outward), (middle_far, outward_far)

    near_block, *far_blocks = along_z(own_block)
    z_blocks = [own_block, near_block] + [jnp.where(inner, *pair) for pair in far_blocks]
    blocks = [
        z_block if j == 0 else shifted(z_block, "y", j)
        for z_block in z_blocks
        for j in range(y_count)
    ]

    query_rows = queries[0].reshape(row_count, H, NOPE + rotary_width)
    nope = query_rows[:, :, :NOPE].reshape(row_count, H * NOPE)
    turning = query_rows[:, :, NOPE:].astype(jnp.float32).transpose(1, 0, 2)
    front, back = turning[:, :, :half_rotary], turning[:, :, half_rotary:]
    token_cosine, token_sine = cosine.T[None], sine.T[None]
    rotated = jnp.concatenate(
        [front * token_cosine - back * token_sine, back * token_cosine + front * token_sine],
        axis=2,
    ).astype(jnp.bfloat16)

    places = jnp.stack(
        [length, z_index.astype(jnp.int32), y_index.astype(jnp.int32), jnp.int32(y_count)]
    )
    prepared = (jnp.concatenate([places, page_table[0]]), nope, rotated, kv_up)
    early = 2 * y_count
    first_blocks = blocks[:early]
    state = attention_call(score_scale, 0, y_count, prepared, first_blocks, (), (), (0, 2))
    state, blocks[-y_count] = lax.optimization_barrier((state, blocks[-y_count]))
    state = attention_call(score_scale, 0, y_count, prepared, first_blocks, state, (), (1, 2))

    column_facts = [block[entry_width:, page_size:] for block in z_blocks]
    column_facts, state = lax.optimization_barrier((column_facts, state))
    residual, *normed = attention_call(
        score_scale,
        2,
        y_count,
        prepared,
        blocks[early:],
        state,
        (out_proj, hidden[0], norm_gain[None, :]),
    )

    slabs_here = expert_in.shape[0]
    experts_here = max(1, slabs_here // 2)
    x_count = lax.axis_size("x")
    plane_devices = x_count * 2 * y_count
    place = jnp.arange(plane_devices, dtype=jnp.int32)
    device_index = (place // y_count) * tok_count + z_index * y_count + place % y_count
    expert_ids = (
        (device_index * slabs_here)[:, None] // 2 + jnp.arange(experts_here, dtype=jnp.int32)
    ).reshape(-1)
    expert_ids = expert_ids.astype(jnp.float32)
    earlier = (offsets[:, None] < offsets[None, :]).astype(jnp.bfloat16)
    group = 2 * CAP
    expert_places = plane_devices * experts_here
    row_ids = jnp.arange(expert_places * group, dtype=jnp.int32)
    spread = (
        row_ids[:, None] // group == jnp.arange(expert_places, dtype=jnp.int32)[None, :]
    ).astype(jnp.bfloat16)
    wanted = (row_ids % group).astype(jnp.float32)[:, None]

    def pair_matrices(first, second):
        codes = []
        weights = []
        for index, fact in enumerate((first, second)):
            match = fact[None, :top_count, :].astype(jnp.float32) == expert_ids[:, None, None]
            named = jnp.any(match, axis=1)
            gates = fact[None, top_count : 2 * top_count, :].astype(jnp.float32)
            weights.append(jnp.sum(jnp.where(match, gates, 0.0), axis=1))
            rank = jnp.dot(
                named.astype(jnp.bfloat16), earlier, preferred_element_type=jnp.float32
            )
            codes.append(jnp.where(named, rank + index * CAP, -1.0))
        code = jnp.concatenate(codes, axis=1).astype(jnp.bfloat16)
        weight = jnp.concatenate(weights, axis=1).astype(jnp.bfloat16)
        chosen = jnp.dot(spread, code, preferred_element_type=jnp.float32) == wanted
        gate_rows = jnp.dot(spread, weight, preferred_element_type=jnp.float32)
        gate_rows = jnp.where(chosen, gate_rows, 0.0).astype(jnp.bfloat16)
        return chosen.astype(jnp.bfloat16), gate_rows.T

    near_matrices = pair_matrices(column_facts[0], column_facts[1])
    far_matrices = pair_matrices(column_facts[2], column_facts[3])

    def exchanged(values):
        return lax.all_to_all(values, PLANE_AXES, split_axis=0, concat_axis=0, tiled=True)

    def all_exchanged(rows):
        rows = rows.reshape(plane_devices, experts_here * group, model_width)
        return exchanged(rows).reshape(expert_places * group, model_width)

    def added(first, second):
        value = first.astype(jnp.float32) + second.astype(jnp.float32)
        return value.astype(jnp.bfloat16)

    def moved(value, pairs):
        return lax.ppermute(value, "z", pairs)

    near = [moved(half, NEAR) for half in normed]
    middle = [moved(half, MIDDLE) for half in normed]
    outward = [moved(half, OUTWARD) for half in middle]
    sent, near[0] = lax.optimization_barrier((normed, near[0]))
    far = [
        [middle, outward],
        [[moved(half, FROM_END) for half in sent], [moved(half, ACROSS) for half in sent]],
    ]
    near_rows = all_exchanged(pack(near_matrices[0], [[normed], [near]]))
    near_rows, far = lax.optimization_barrier((near_rows, far))
    far_rows = all_exchanged(pack(far_matrices[0], far))
    near_rows = experts(near_rows, expert_in, expert_out, experts_here, group)
    near_rows, far_rows = lax.optimization_barrier((near_rows, far_rows))
    near_rows = all_exchanged(near_rows)
    far_rows = experts(far_rows, expert_in, expert_out, experts_here, group)
    near_rows, far_rows = lax.optimization_barrier((near_rows, far_rows))
    far_rows = all_exchanged(far_rows)

    half_shape = jax.ShapeDtypeStruct((row_count, model_width // 2), jnp.bfloat16)
    whole_shape = jax.ShapeDtypeStruct((row_count, model_width), jnp.float32)
    own_part, *near_parts = combine(
        near_matrices[1], near_rows, [whole_shape] + [half_shape] * 2
    )
    near_arrived = [moved(part, NEAR) for part in near_parts]
    near_arrived, far_rows = lax.optimization_barrier((near_arrived, far_rows))
    part_shape = jax.ShapeDtypeStruct((row_count, model_width), jnp.bfloat16)
    middle_part, far_part = combine(far_matrices[1], far_rows, [part_shape] * 2)
    middle_arrived = moved(middle_part, INWARD)
    far_arrived = [moved(far_part, TO_END), moved(far_part, ACROSS)]
    middle_arrived = moved(added(middle_part, middle_arrived), MIDDLE)
    layer_out = pl.pallas_call(
        finish_kernel,
        out_shape=jax.ShapeDtypeStruct((row_count, model_width), jnp.bfloat16),
        compiler_params=pltpu.CompilerParams(vmem_limit_bytes=40 * MIB),
    )(residual, own_part, *near_arrived, middle_arrived, *far_arrived)
    return (layer_out[None], new_entries.T[None])


def solution(mesh):
    req_count, tok_count = mesh.devices.shape
    devices = mesh.devices.reshape(req_count // 2, 2, PLANES, tok_count // PLANES)
    fine = Mesh(devices, ("x", "core", "z", "y"))
    req = ("x", "core")
    tok = ("z", "y")
    placed = (
        P(req, tok, None),
        P(req, tok, None),
        P(req, tok, None),
        P(req, tok, None, None),
        P(req, None),
        P(req),
        P(req, tok, None),
        P(req, tok, None),
        P(),
        P(),
        P(),
        P(),
        P(("x", "core", "z", "y"), None, None),
        P(("x", "core", "z", "y"), None, None),
    )
    return jax.shard_map(
        local,
        mesh=fine,
        in_specs=placed,
        out_specs=(P(req, tok, None), P(req, tok, None)),
        check_vma=False,
    )
```

```python
import functools
import math

import jax
import jax.numpy as jnp
from jax import lax
from jax.experimental import pallas as pl
from jax.experimental.pallas import tpu as pltpu
from jax.sharding import Mesh
from jax.sharding import PartitionSpec as P

H = 16
NOPE = 128
VD = 128
CAP = 14
PLANES = 4
PAIR = 2
GROUPS = 2
PARTS = 2

epsilon = 1e-06
theta_base = 10000.0
hidden_score = -1e30
PLANE_AXES = ("x", "core", "y")
MIB = 1 << 20
FACT_ROWS = 16
NEAR = [(0, 1), (1, 0), (2, 3), (3, 2)]
MIDDLE = [(1, 2), (2, 1)]
OUTWARD = [(1, 0), (2, 3)]
INWARD = [(0, 1), (3, 2)]


def shifted(values, axis, step):
    count = lax.axis_size(axis)
    return lax.ppermute(values, axis, [(i, (i + step) % count) for i in range(count)])


def entries_kernel(fresh_ref, page_ref, facts_ref, cos_ref, sin_ref, gain_ref, block_ref, new_ref):
    latent_width = gain_ref.shape[0] * gain_ref.shape[1]
    entry_width = fresh_ref.shape[0]
    half = cos_ref.shape[0]
    rows = fresh_ref.shape[1]
    raw = fresh_ref[:latent_width, :].astype(jnp.float32)
    mean = jnp.mean(raw * raw, axis=0, keepdims=True)
    gain = jnp.concatenate(
        [
            jnp.broadcast_to(gain_ref[i : i + 1, :], (rows, gain_ref.shape[1])).T
            for i in range(gain_ref.shape[0])
        ],
        axis=0,
    )
    latent = (raw * lax.rsqrt(mean + epsilon) * gain).astype(jnp.bfloat16)
    front = fresh_ref[latent_width : latent_width + half, :].astype(jnp.float32)
    back = fresh_ref[latent_width + half :, :].astype(jnp.float32)
    cosine = cos_ref[...]
    sine = sin_ref[...]
    turned_front = (front * cosine - back * sine).astype(jnp.bfloat16)
    turned_back = (back * cosine + front * sine).astype(jnp.bfloat16)
    new_ref[:latent_width, :] = latent
    new_ref[latent_width : latent_width + half, :] = turned_front
    new_ref[latent_width + half :, :] = turned_back
    block_ref[:entry_width, :rows] = page_ref[...]
    block_ref[:latent_width, rows:] = latent
    block_ref[latent_width : latent_width + half, rows:] = turned_front
    block_ref[latent_width + half : entry_width, rows:] = turned_back
    block_ref[entry_width:, rows:] = facts_ref[...]
    block_ref[entry_width:, :rows] = facts_ref[...]


def attend(nope_ref, rotated_ref, up_ref, facts_ref, marks_ref, keys_ref, score_scale):
    latent_width = up_ref.shape[0]
    head_width = NOPE + VD
    keys_latent = keys_ref[:latent_width, :]
    keys_rotated = keys_ref[latent_width:, :]
    rows = nope_ref.shape[0]
    first_row = (facts_ref[1] * facts_ref[3] + facts_ref[2]) * rows
    query_rows = lax.broadcasted_iota(jnp.int32, (PAIR * rows, 1), 0)
    allowed = marks_ref[...] <= lax.rem(query_rows, rows) + first_row
    scores = []
    for group in range(GROUPS):
        heads = range(group * PAIR, (group + 1) * PAIR)
        query_latent = jnp.concatenate(
            [
                lax.dot_general(
                    nope_ref[:, i * NOPE : (i + 1) * NOPE],
                    up_ref[:, i * head_width : i * head_width + NOPE],
                    (((1,), (1,)), ((), ())),
                    preferred_element_type=jnp.float32,
                ).astype(jnp.bfloat16)
                for i in heads
            ],
            axis=0,
        )
        query_rotated = jnp.concatenate([rotated_ref[i] for i in heads], axis=0)
        value = jnp.dot(query_latent, keys_latent, preferred_element_type=jnp.float32)
        value = value + jnp.dot(query_rotated, keys_rotated, preferred_element_type=jnp.float32)
        scores.append(jnp.where(allowed, value, hidden_score))
    results = []
    for group in range(GROUPS):
        highest = jnp.max(scores[group], axis=1, keepdims=True)
        soft = jnp.exp((scores[group] - highest) * score_scale)
        totals = jnp.sum(soft, axis=1, keepdims=True)
        mixed = lax.dot_general(
            soft.astype(jnp.bfloat16),
            keys_latent,
            (((1,), (1,)), ((), ())),
            preferred_element_type=jnp.float32,
        )
        results.append((highest, totals, mixed))
    return results


def fill_keys(facts_ref, block_refs, keys_ref, marks_ref, first_slot, y_count, rows):
    width = block_refs[0].shape[1]
    length, z_index, y_index = facts_ref[0], facts_ref[1], facts_ref[2]
    low = z_index < 2
    pool = facts_ref.shape[0] - 4
    page_size = width - rows
    for index, block_ref in enumerate(block_refs):
        keys_ref[:, index * width : (index + 1) * width] = block_ref[: keys_ref.shape[0], :]
        slot = first_slot + index // y_count
        z_source = (
            z_index,
            z_index + 1 - 2 * lax.rem(z_index, 2),
            jnp.where(low, 2, 1),
            jnp.where(low, 3, 0),
        )[slot]
        y_source = lax.rem(y_index + y_count - index % y_count, y_count)
        source = z_source * y_count + y_source
        logical = jnp.int32(0)
        for place in range(pool):
            logical = logical + jnp.where(facts_ref[4 + place] == source, place, 0)
        cached = lax.broadcasted_iota(jnp.int32, (1, page_size), 1) + logical * page_size
        marks_ref[:, index * width : index * width + page_size] = jnp.where(
            cached < length, -1, 1 << 30
        )
        marks_ref[:, index * width + page_size : (index + 1) * width] = (
            lax.broadcasted_iota(jnp.int32, (1, rows), 1) + source * rows
        )


def merged(result, group, old_refs, score_scale):
    highest, totals, mixed = result
    old_highest, old_totals, old_mixed = [ref[group] for ref in old_refs]
    top = jnp.maximum(highest, old_highest)
    fresh = jnp.exp((highest - top) * score_scale)
    fading = jnp.exp((old_highest - top) * score_scale)
    return top, totals * fresh + old_totals * fading, mixed * fresh + old_mixed * fading


def first_attention_kernel(score_scale, first_slot, y_count, block_count, *refs):
    facts_ref, nope_ref, rotated_ref, up_ref = refs[:4]
    block_refs = refs[4 : 4 + block_count]
    highest_ref, totals_ref, mixed_ref, keys_ref, marks_ref = refs[-5:]

    @pl.when(pl.program_id(0) == 0)
    def _():
        fill_keys(
            facts_ref, block_refs, keys_ref, marks_ref, first_slot, y_count, nope_ref.shape[0]
        )

    results = attend(nope_ref, rotated_ref, up_ref, facts_ref, marks_ref, keys_ref, score_scale)
    for group, (highest, totals, mixed) in enumerate(results):
        highest_ref[group] = highest
        totals_ref[group] = totals
        mixed_ref[group] = mixed


def last_attention_kernel(score_scale, first_slot, y_count, block_count, *refs):
    facts_ref, nope_ref, rotated_ref, up_ref = refs[:4]
    block_refs = refs[4 : 4 + block_count]
    old_refs = refs[4 + block_count : 7 + block_count]
    proj_ref, hidden_ref, gain_ref = refs[7 + block_count : 10 + block_count]
    residual_ref, left_ref, right_ref, keys_ref, marks_ref, total_ref = refs[10 + block_count :]
    step = pl.program_id(0)
    rows = hidden_ref.shape[0]
    head_width = NOPE + VD

    @pl.when(step == 0)
    def _():
        fill_keys(facts_ref, block_refs, keys_ref, marks_ref, first_slot, y_count, rows)

    results = attend(nope_ref, rotated_ref, up_ref, facts_ref, marks_ref, keys_ref, score_scale)
    outs = []
    for group, result in enumerate(results):
        _, totals, mixed = merged(result, group, old_refs, score_scale)
        mixed = (mixed / totals).astype(jnp.bfloat16)
        for i in range(PAIR):
            head = group * PAIR + i
            outs.append(
                jnp.dot(
                    mixed[i * rows : (i + 1) * rows],
                    up_ref[:, head * head_width + NOPE : (head + 1) * head_width],
                    preferred_element_type=jnp.float32,
                ).astype(jnp.bfloat16)
            )
    head_out = jnp.concatenate(outs, axis=1)
    part = jnp.dot(head_out, proj_ref[...], preferred_element_type=jnp.float32)

    @pl.when(step == 0)
    def _():
        total_ref[...] = part

    @pl.when(step > 0)
    def _():
        total_ref[...] += part

    @pl.when(step == pl.num_programs(0) - 1)
    def _():
        residual = hidden_ref[...].astype(jnp.float32) + total_ref[...]
        residual_ref[...] = residual
        mean = jnp.mean(residual * residual, axis=1, keepdims=True)
        normed = (residual * lax.rsqrt(mean + epsilon) * gain_ref[...]).astype(jnp.bfloat16)
        left_ref[...] = normed[:, : left_ref.shape[1]]
        right_ref[...] = normed[:, left_ref.shape[1] :]


def attention_call(score_scale, first_slot, y_count, queries, blocks, old, tail, part=None):
    facts, nope, rotated, up = queries
    rows = nope.shape[0]
    latent_width = up.shape[0]
    block_height, width = blocks[0].shape
    keys = width * len(blocks)
    rotary_width = rotated.shape[2]
    heads = PAIR * GROUPS
    whole = lambda *shape: pl.BlockSpec(shape, lambda s: (0,) * len(shape))
    index, count = part or (0, 1)
    steps = H // heads // count
    start = index * steps
    state_specs = [
        pl.BlockSpec((GROUPS, PAIR * rows, size), lambda s: (s + start, 0, 0))
        for size in (1, 1, latent_width)
    ]
    in_specs = [
        pl.BlockSpec(memory_space=pltpu.SMEM),
        pl.BlockSpec((rows, heads * NOPE), lambda s: (0, s + start)),
        pl.BlockSpec((heads, rows, rotary_width), lambda s: (s + start, 0, 0)),
        pl.BlockSpec((latent_width, heads * (NOPE + VD)), lambda s: (0, s + start)),
    ] + [whole(block_height, width)] * len(blocks)
    scratch = [
        pltpu.VMEM((latent_width + rotary_width, keys), jnp.bfloat16),
        pltpu.VMEM((1, keys), jnp.int32),
    ]
    aliases = {}
    if old and part:
        aliases = {len(in_specs) + i: i for i in range(len(old))}
        in_specs += [pl.BlockSpec(memory_space=pl.ANY)] * len(old)
    elif old:
        in_specs += state_specs
    if tail:
        proj, hidden, gain = tail
        model_width = hidden.shape[1]
        kernel = last_attention_kernel
        in_specs += [
            pl.BlockSpec((heads * VD, model_width), lambda s: (s, 0)),
            whole(rows, model_width),
            whole(1, model_width),
        ]
        out_specs = [whole(rows, model_width)] + [whole(rows, model_width // 2)] * 2
        out_shape = [
            jax.ShapeDtypeStruct((rows, model_width), jnp.float32),
            jax.ShapeDtypeStruct((rows, model_width // 2), jnp.bfloat16),
            jax.ShapeDtypeStruct((rows, model_width // 2), jnp.bfloat16),
        ]
        scratch.append(pltpu.VMEM((rows, model_width), jnp.float32))
    else:
        kernel = first_attention_kernel
        out_specs = state_specs
        out_shape = [
            jax.ShapeDtypeStruct((H // PAIR, PAIR * rows, size), jnp.float32)
            for size in (1, 1, latent_width)
        ]
    return pl.pallas_call(
        functools.partial(kernel, score_scale, first_slot, y_count, len(blocks)),
        grid=(steps,),
        in_specs=in_specs,
        out_specs=out_specs,
        out_shape=out_shape,
        scratch_shapes=scratch,
        input_output_aliases=aliases,
        compiler_params=pltpu.CompilerParams(vmem_limit_bytes=56 * MIB),
        cost_estimate=pl.CostEstimate(
            flops=2 * H * rows * keys * (2 * latent_width + rotary_width) // count,
            bytes_accessed=16 * MIB // count,
            transcendentals=H * rows * keys // count,
        ),
    )(facts, nope, rotated, up, *blocks, *old, *tail)


def experts_kernel(slabs_each, sorting, x_ref, *refs):
    if sorting:
        take_ref, put_ref = refs[:2]
        refs = refs[2:]
    in_refs = refs[:PARTS]
    out_weight_refs = refs[PARTS : 2 * PARTS]
    result_ref = refs[2 * PARTS]
    rows_ref, total_ref = refs[2 * PARTS + 1 :]
    expert = pl.program_id(0)
    slab = pl.program_id(1)

    @pl.when(slab == 0)
    def _():
        if sorting:
            rows_ref[...] = jnp.dot(
                take_ref[0], x_ref[...], preferred_element_type=jnp.float32
            ).astype(jnp.bfloat16)
        else:
            rows_ref[...] = x_ref[...]

    depth = in_refs[0].shape[1]
    projected = None
    for index, in_ref in enumerate(in_refs):
        piece = jnp.dot(
            rows_ref[:, index * depth : (index + 1) * depth],
            in_ref[0],
            preferred_element_type=jnp.float32,
        )
        projected = piece if projected is None else projected + piece
    piece_half = out_weight_refs[0].shape[1]
    half = piece_half * PARTS
    active = (jax.nn.silu(projected[:, :half]) * projected[:, half:]).astype(jnp.bfloat16)
    part = None
    for index, out_weight_ref in enumerate(out_weight_refs):
        piece = jnp.dot(
            active[:, index * piece_half : (index + 1) * piece_half],
            out_weight_ref[0],
            preferred_element_type=jnp.float32,
        )
        part = piece if part is None else part + piece

    if slabs_each > 1:

        @pl.when(slab == 0)
        def _():
            total_ref[...] = part

    @pl.when(slab == slabs_each - 1)
    def _():
        value = part
        if slabs_each > 1:
            value = value + total_ref[...]
        value = value.astype(jnp.bfloat16)
        if sorting:
            value = jnp.dot(put_ref[0], value, preferred_element_type=jnp.float32).astype(
                jnp.bfloat16
            )

            @pl.when(expert == 0)
            def _():
                result_ref[...] = value

            @pl.when(expert > 0)
            def _():
                result_ref[...] += value
        else:
            result_ref[...] = value


def experts(x, expert_in, expert_out, experts_here, group):
    rows, width = x.shape
    slabs_each = expert_in.shape[0] // experts_here
    half = expert_out.shape[1]
    each = rows // experts_here
    sorting = experts_here > 1
    operands = [x]
    in_specs = [pl.BlockSpec((rows, width), lambda e, s: (0, 0))]
    if sorting:
        place = jnp.arange(each, dtype=jnp.int32)
        target = (
            (place // group * experts_here)[None, :]
            + jnp.arange(experts_here, dtype=jnp.int32)[:, None]
        ) * group + (place % group)[None, :]
        column = jnp.arange(rows, dtype=jnp.int32)
        take = (target[:, :, None] == column[None, None, :]).astype(jnp.bfloat16)
        put = (target[:, None, :] == column[None, :, None]).astype(jnp.bfloat16)
        operands += [take, put]
        in_specs += [
            pl.BlockSpec((1, each, rows), lambda e, s: (e, 0, 0)),
            pl.BlockSpec((1, rows, each), lambda e, s: (e, 0, 0)),
        ]

    def piece(height, columns, index):
        return pl.BlockSpec((1, height, columns), lambda e, s: (e * slabs_each + s, index, 0))

    operands += [expert_in] * PARTS + [expert_out] * PARTS
    in_specs += [piece(width // PARTS, 2 * half, i) for i in range(PARTS)]
    in_specs += [piece(half // PARTS, width, i) for i in range(PARTS)]
    return pl.pallas_call(
        functools.partial(experts_kernel, slabs_each, sorting),
        grid=(experts_here, slabs_each),
        in_specs=in_specs,
        out_specs=pl.BlockSpec((rows, width), lambda e, s: (0, 0)),
        out_shape=jax.ShapeDtypeStruct((rows, width), jnp.bfloat16),
        scratch_shapes=[
            pltpu.VMEM((each, width), jnp.bfloat16),
            pltpu.VMEM((each, width), jnp.float32),
        ],
        compiler_params=pltpu.CompilerParams(vmem_limit_bytes=58 * MIB),
        cost_estimate=pl.CostEstimate(
            flops=6 * rows * width * half * slabs_each,
            bytes_accessed=2 * 3 * width * half * experts_here * slabs_each,
            transcendentals=rows * half,
        ),
    )(*operands)


def pack_kernel(layers, place_ref, *refs):
    *token_refs, result_ref = refs
    sides = len(token_refs) // (2 * layers)
    width = token_refs[0].shape[1]
    for side in range(sides):
        blocks = []
        for block in range(2):
            value = None
            for layer in range(layers):
                piece = token_refs[(block * layers + layer) * sides + side][...]
                value = piece if value is None else value + piece
            blocks.append(value)
        tokens = jnp.concatenate(blocks, axis=0)
        result_ref[:, side * width : (side + 1) * width] = jnp.dot(
            place_ref[...], tokens, preferred_element_type=jnp.float32
        ).astype(jnp.bfloat16)


def pack(placing, blocks):
    layers = len(blocks[0])
    operands = [half for block in blocks for layer in block for half in layer]
    rows, tokens = placing.shape
    width = sum(half.shape[1] for half in blocks[0][0])
    return pl.pallas_call(
        functools.partial(pack_kernel, layers),
        out_shape=jax.ShapeDtypeStruct((rows, width), jnp.bfloat16),
        compiler_params=pltpu.CompilerParams(vmem_limit_bytes=40 * MIB),
        cost_estimate=pl.CostEstimate(
            flops=2 * rows * tokens * width, bytes_accessed=6 * rows * width, transcendentals=0
        ),
    )(placing, *operands)


def combine_kernel(weights_ref, rows_ref, *out_refs):
    value = jnp.dot(weights_ref[...], rows_ref[...], preferred_element_type=jnp.float32)
    row = 0
    column = 0
    for out_ref in out_refs:
        height, width = out_ref.shape
        out_ref[...] = value[row : row + height, column : column + width].astype(out_ref.dtype)
        column += width
        if column == value.shape[1]:
            row, column = row + height, 0


def combine(weights, rows, out_shape):
    return pl.pallas_call(
        combine_kernel,
        out_shape=out_shape,
        compiler_params=pltpu.CompilerParams(vmem_limit_bytes=40 * MIB),
        cost_estimate=pl.CostEstimate(
            flops=2 * weights.shape[0] * rows.size,
            bytes_accessed=4 * rows.size,
            transcendentals=0,
        ),
    )(weights, rows)


def finish_kernel(residual_ref, own_ref, *refs):
    *part_refs, out_ref = refs
    width = part_refs[0].shape[1]
    for side in range(2):
        columns = slice(side * width, (side + 1) * width)
        value = residual_ref[:, columns] + own_ref[:, columns]
        for part_ref in part_refs[side::2]:
            value = value + part_ref[...].astype(jnp.float32)
        out_ref[:, columns] = value.astype(out_ref.dtype)


def local(
    hidden,
    queries,
    fresh_latent,
    latent_cache,
    page_table,
    cache_lengths,
    routes,
    route_gates,
    kv_up,
    out_proj,
    latent_gain,
    norm_gain,
    expert_in,
    expert_out,
):
    row_count = hidden.shape[1]
    model_width = hidden.shape[2]
    latent_width = latent_gain.shape[0]
    entry_width = fresh_latent.shape[2]
    rotary_width = entry_width - latent_width
    half_rotary = rotary_width // 2
    score_scale = 1.0 / math.sqrt(NOPE + rotary_width)
    length = cache_lengths[0]
    y_count = lax.axis_size("y")
    z_index = lax.axis_index("z")
    y_index = lax.axis_index("y")
    tok_index = z_index * y_count + y_index
    tok_count = PLANES * y_count

    first_row = tok_index * row_count
    offsets = jnp.arange(row_count, dtype=jnp.int32)
    positions = (length + first_row + offsets).astype(jnp.float32)
    frequency = theta_base ** (-jnp.arange(half_rotary, dtype=jnp.float32) * 2.0 / rotary_width)
    angles = frequency[:, None] * positions[None, :]
    cosine = jnp.cos(angles)
    sine = jnp.sin(angles)
    page_size = latent_cache.shape[2]
    top_count = routes.shape[2]
    own_facts = jnp.concatenate(
        [
            routes[0].T.astype(jnp.bfloat16),
            route_gates[0].T.astype(jnp.bfloat16),
            jnp.zeros((FACT_ROWS - 2 * top_count, row_count), jnp.bfloat16),
        ],
        axis=0,
    )
    own_block, new_entries = pl.pallas_call(
        entries_kernel,
        out_shape=[
            jax.ShapeDtypeStruct((entry_width + FACT_ROWS, page_size + row_count), jnp.bfloat16),
            jax.ShapeDtypeStruct((entry_width, row_count), jnp.bfloat16),
        ],
    )(
        fresh_latent[0].T,
        latent_cache[0, 0].T,
        own_facts,
        cosine,
        sine,
        latent_gain.reshape(latent_width // row_count, row_count),
    )

    inner = jnp.logical_or(z_index == 1, z_index == 2)

    def along_z(values):
        near = lax.ppermute(values, "z", NEAR)
        middle = lax.ppermute(values, "z", MIDDLE)
        middle_far = lax.ppermute(near, "z", MIDDLE)
        outward = lax.ppermute(middle, "z", OUTWARD)
        outward_far = lax.ppermute(middle_far, "z", OUTWARD)
        return near, (middle, outward), (middle_far, outward_far)

    near_block, *far_blocks = along_z(own_block)
    z_blocks = [own_block, near_block] + [jnp.where(inner, *pair) for pair in far_blocks]
    blocks = [
        z_block if j == 0 else shifted(z_block, "y", j)
        for z_block in z_blocks
        for j in range(y_count)
    ]

    query_rows = queries[0].reshape(row_count, H, NOPE + rotary_width)
    nope = query_rows[:, :, :NOPE].reshape(row_count, H * NOPE)
    turning = query_rows[:, :, NOPE:].astype(jnp.float32).transpose(1, 0, 2)
    front, back = turning[:, :, :half_rotary], turning[:, :, half_rotary:]
    token_cosine, token_sine = cosine.T[None], sine.T[None]
    rotated = jnp.concatenate(
        [front * token_cosine - back * token_sine, back * token_cosine + front * token_sine],
        axis=2,
    ).astype(jnp.bfloat16)

    places = jnp.stack(
        [length, z_index.astype(jnp.int32), y_index.astype(jnp.int32), jnp.int32(y_count)]
    )
    prepared = (jnp.concatenate([places, page_table[0]]), nope, rotated, kv_up)
    early = 2 * y_count
    first_blocks = blocks[:early]
    state = attention_call(score_scale, 0, y_count, prepared, first_blocks, (), (), (0, 2))
    state, blocks[-y_count] = lax.optimization_barrier((state, blocks[-y_count]))
    state = attention_call(score_scale, 0, y_count, prepared, first_blocks, state, (), (1, 2))

    column_facts = [block[entry_width:, page_size:] for block in z_blocks]
    column_facts, state = lax.optimization_barrier((column_facts, state))
    residual, *normed = attention_call(
        score_scale,
        2,
        y_count,
        prepared,
        blocks[early:],
        state,
        (out_proj, hidden[0], norm_gain[None, :]),
    )

    slabs_here = expert_in.shape[0]
    experts_here = max(1, slabs_here // 2)
    x_count = lax.axis_size("x")
    plane_devices = x_count * 2 * y_count
    place = jnp.arange(plane_devices, dtype=jnp.int32)
    device_index = (place // y_count) * tok_count + z_index * y_count + place % y_count
    expert_ids = (
        (device_index * slabs_here)[:, None] // 2 + jnp.arange(experts_here, dtype=jnp.int32)
    ).reshape(-1)
    expert_ids = expert_ids.astype(jnp.float32)
    earlier = (offsets[:, None] < offsets[None, :]).astype(jnp.bfloat16)
    group = 2 * CAP
    expert_places = plane_devices * experts_here
    row_ids = jnp.arange(expert_places * group, dtype=jnp.int32)
    spread = (
        row_ids[:, None] // group == jnp.arange(expert_places, dtype=jnp.int32)[None, :]
    ).astype(jnp.bfloat16)
    wanted = (row_ids % group).astype(jnp.float32)[:, None]

    def pair_matrices(first, second):
        codes = []
        weights = []
        for index, fact in enumerate((first, second)):
            match = fact[None, :top_count, :].astype(jnp.float32) == expert_ids[:, None, None]
            named = jnp.any(match, axis=1)
            gates = fact[None, top_count : 2 * top_count, :].astype(jnp.float32)
            weights.append(jnp.sum(jnp.where(match, gates, 0.0), axis=1))
            rank = jnp.dot(
                named.astype(jnp.bfloat16), earlier, preferred_element_type=jnp.float32
            )
            codes.append(jnp.where(named, rank + index * CAP, -1.0))
        code = jnp.concatenate(codes, axis=1).astype(jnp.bfloat16)
        weight = jnp.concatenate(weights, axis=1).astype(jnp.bfloat16)
        chosen = jnp.dot(spread, code, preferred_element_type=jnp.float32) == wanted
        gate_rows = jnp.dot(spread, weight, preferred_element_type=jnp.float32)
        gate_rows = jnp.where(chosen, gate_rows, 0.0).astype(jnp.bfloat16)
        return chosen.astype(jnp.bfloat16), gate_rows.T

    near_matrices = pair_matrices(column_facts[0], column_facts[1])
    far_matrices = pair_matrices(column_facts[2], column_facts[3])

    def exchanged(values):
        return lax.all_to_all(values, PLANE_AXES, split_axis=0, concat_axis=0, tiled=True)

    def all_exchanged(rows):
        rows = rows.reshape(plane_devices, experts_here * group, model_width)
        return exchanged(rows).reshape(expert_places * group, model_width)

    near, *far = zip(*[along_z(half) for half in normed])
    (middle, outward), (other_middle, other_outward) = far[0]
    middle_far = far[1][0][0]
    near, middle, other_middle, outward, middle_far = lax.optimization_barrier(
        (near, middle, other_middle, outward, middle_far)
    )
    far[1] = [(middle_far, far[1][0][1]), far[1][1]]
    far[0] = [(middle, outward), (other_middle, other_outward)]
    near_rows = all_exchanged(pack(near_matrices[0], [[normed], [near]]))
    far = [list(zip(*block)) for block in far]
    near_rows, far = lax.optimization_barrier((near_rows, far))
    far_rows = all_exchanged(pack(far_matrices[0], far))
    near_rows = experts(near_rows, expert_in, expert_out, experts_here, group)
    near_rows, far_rows = lax.optimization_barrier((near_rows, far_rows))
    near_rows = all_exchanged(near_rows)
    far_rows = experts(far_rows, expert_in, expert_out, experts_here, group)
    near_rows, far_rows = lax.optimization_barrier((near_rows, far_rows))
    far_rows = all_exchanged(far_rows)

    def added(first, second):
        value = first.astype(jnp.float32) + second.astype(jnp.float32)
        return value.astype(jnp.bfloat16)

    def moved(value, pairs):
        return lax.ppermute(value, "z", pairs)

    half_shape = jax.ShapeDtypeStruct((row_count, model_width // 2), jnp.bfloat16)
    whole_shape = jax.ShapeDtypeStruct((row_count, model_width), jnp.float32)
    own_part, *near_parts = combine(
        near_matrices[1], near_rows, [whole_shape] + [half_shape] * 2
    )
    near_arrived = [moved(part, NEAR) for part in near_parts]
    near_arrived, far_rows = lax.optimization_barrier((near_arrived, far_rows))
    returned = combine(far_matrices[1], far_rows, [half_shape] * 4)
    middle_parts, far_parts = returned[:2], returned[2:]
    far_arrived = [moved(part, INWARD) for part in far_parts]
    middle_parts, far_arrived[1] = lax.optimization_barrier((middle_parts, far_arrived[1]))
    middle_arrived = [moved(part, INWARD) for part in middle_parts]
    far_arrived = [moved(added(*pair), MIDDLE) for pair in zip(far_parts, far_arrived)]
    middle_arrived = [moved(added(*pair), MIDDLE) for pair in zip(middle_parts, middle_arrived)]
    far_arrived = [moved(part, OUTWARD) for part in far_arrived]
    layer_out = pl.pallas_call(
        finish_kernel,
        out_shape=jax.ShapeDtypeStruct((row_count, model_width), jnp.bfloat16),
        compiler_params=pltpu.CompilerParams(vmem_limit_bytes=40 * MIB),
    )(residual, own_part, *near_arrived, *middle_arrived, *far_arrived)
    return (layer_out[None], new_entries.T[None])


def solution(mesh):
    req_count, tok_count = mesh.devices.shape
    devices = mesh.devices.reshape(req_count // 2, 2, PLANES, tok_count // PLANES)
    fine = Mesh(devices, ("x", "core", "z", "y"))
    req = ("x", "core")
    tok = ("z", "y")
    placed = (
        P(req, tok, None),
        P(req, tok, None),
        P(req, tok, None),
        P(req, tok, None, None),
        P(req, None),
        P(req),
        P(req, tok, None),
        P(req, tok, None),
        P(),
        P(),
        P(),
        P(),
        P(("x", "core", "z", "y"), None, None),
        P(("x", "core", "z", "y"), None, None),
    )
    return jax.shard_map(
        local,
        mesh=fine,
        in_specs=placed,
        out_specs=(P(req, tok, None), P(req, tok, None)),
        check_vma=False,
    )
```

```python
import functools
import math

import jax
import jax.numpy as jnp
from jax import lax
from jax.experimental import pallas as pl
from jax.experimental.pallas import tpu as pltpu
from jax.sharding import Mesh
from jax.sharding import PartitionSpec as P

H = 16
NOPE = 128
VD = 128
CAP = 14
PLANES = 4
PAIR = 2
GROUPS = 2
PARTS = 2

epsilon = 1e-06
theta_base = 10000.0
hidden_score = -1e30
PLANE_AXES = ("x", "core", "y")
MIB = 1 << 20
FACT_ROWS = 16
NEAR = [(0, 1), (1, 0), (2, 3), (3, 2)]
MIDDLE = [(1, 2), (2, 1)]
OUTWARD = [(1, 0), (2, 3)]
INWARD = [(0, 1), (3, 2)]


def shifted(values, axis, step):
    count = lax.axis_size(axis)
    return lax.ppermute(values, axis, [(i, (i + step) % count) for i in range(count)])


def entries_kernel(fresh_ref, page_ref, facts_ref, cos_ref, sin_ref, gain_ref, block_ref, new_ref):
    latent_width = gain_ref.shape[0] * gain_ref.shape[1]
    entry_width = fresh_ref.shape[0]
    half = cos_ref.shape[0]
    rows = fresh_ref.shape[1]
    raw = fresh_ref[:latent_width, :].astype(jnp.float32)
    mean = jnp.mean(raw * raw, axis=0, keepdims=True)
    gain = jnp.concatenate(
        [
            jnp.broadcast_to(gain_ref[i : i + 1, :], (rows, gain_ref.shape[1])).T
            for i in range(gain_ref.shape[0])
        ],
        axis=0,
    )
    latent = (raw * lax.rsqrt(mean + epsilon) * gain).astype(jnp.bfloat16)
    front = fresh_ref[latent_width : latent_width + half, :].astype(jnp.float32)
    back = fresh_ref[latent_width + half :, :].astype(jnp.float32)
    cosine = cos_ref[...]
    sine = sin_ref[...]
    turned_front = (front * cosine - back * sine).astype(jnp.bfloat16)
    turned_back = (back * cosine + front * sine).astype(jnp.bfloat16)
    new_ref[:latent_width, :] = latent
    new_ref[latent_width : latent_width + half, :] = turned_front
    new_ref[latent_width + half :, :] = turned_back
    block_ref[:entry_width, :rows] = page_ref[...]
    block_ref[:latent_width, rows:] = latent
    block_ref[latent_width : latent_width + half, rows:] = turned_front
    block_ref[latent_width + half : entry_width, rows:] = turned_back
    block_ref[entry_width:, rows:] = facts_ref[...]
    block_ref[entry_width:, :rows] = facts_ref[...]


def attend(nope_ref, rotated_ref, up_ref, facts_ref, marks_ref, keys_ref, score_scale):
    latent_width = up_ref.shape[0]
    head_width = NOPE + VD
    keys_latent = keys_ref[:latent_width, :]
    keys_rotated = keys_ref[latent_width:, :]
    rows = nope_ref.shape[0]
    first_row = (facts_ref[1] * facts_ref[3] + facts_ref[2]) * rows
    query_rows = lax.broadcasted_iota(jnp.int32, (PAIR * rows, 1), 0)
    allowed = marks_ref[...] <= lax.rem(query_rows, rows) + first_row
    scores = []
    for group in range(GROUPS):
        heads = range(group * PAIR, (group + 1) * PAIR)
        query_latent = jnp.concatenate(
            [
                lax.dot_general(
                    nope_ref[:, i * NOPE : (i + 1) * NOPE],
                    up_ref[:, i * head_width : i * head_width + NOPE],
                    (((1,), (1,)), ((), ())),
                    preferred_element_type=jnp.float32,
                ).astype(jnp.bfloat16)
                for i in heads
            ],
            axis=0,
        )
        query_rotated = jnp.concatenate([rotated_ref[i] for i in heads], axis=0)
        value = jnp.dot(query_latent, keys_latent, preferred_element_type=jnp.float32)
        value = value + jnp.dot(query_rotated, keys_rotated, preferred_element_type=jnp.float32)
        scores.append(jnp.where(allowed, value, hidden_score))
    results = []
    for group in range(GROUPS):
        highest = jnp.max(scores[group], axis=1, keepdims=True)
        soft = jnp.exp((scores[group] - highest) * score_scale)
        totals = jnp.sum(soft, axis=1, keepdims=True)
        mixed = lax.dot_general(
            soft.astype(jnp.bfloat16),
            keys_latent,
            (((1,), (1,)), ((), ())),
            preferred_element_type=jnp.float32,
        )
        results.append((highest, totals, mixed))
    return results


def fill_keys(facts_ref, block_refs, keys_ref, marks_ref, first_slot, y_count, rows):
    width = block_refs[0].shape[1]
    length, z_index, y_index = facts_ref[0], facts_ref[1], facts_ref[2]
    low = z_index < 2
    pool = facts_ref.shape[0] - 4
    page_size = width - rows
    for index, block_ref in enumerate(block_refs):
        keys_ref[:, index * width : (index + 1) * width] = block_ref[: keys_ref.shape[0], :]
        slot = first_slot + index // y_count
        z_source = (
            z_index,
            z_index + 1 - 2 * lax.rem(z_index, 2),
            jnp.where(low, 2, 1),
            jnp.where(low, 3, 0),
        )[slot]
        y_source = lax.rem(y_index + y_count - index % y_count, y_count)
        source = z_source * y_count + y_source
        logical = jnp.int32(0)
        for place in range(pool):
            logical = logical + jnp.where(facts_ref[4 + place] == source, place, 0)
        cached = lax.broadcasted_iota(jnp.int32, (1, page_size), 1) + logical * page_size
        marks_ref[:, index * width : index * width + page_size] = jnp.where(
            cached < length, -1, 1 << 30
        )
        marks_ref[:, index * width + page_size : (index + 1) * width] = (
            lax.broadcasted_iota(jnp.int32, (1, rows), 1) + source * rows
        )


def merged(result, group, old_refs, score_scale):
    highest, totals, mixed = result
    old_highest, old_totals, old_mixed = [ref[group] for ref in old_refs]
    top = jnp.maximum(highest, old_highest)
    fresh = jnp.exp((highest - top) * score_scale)
    fading = jnp.exp((old_highest - top) * score_scale)
    return top, totals * fresh + old_totals * fading, mixed * fresh + old_mixed * fading


def first_attention_kernel(score_scale, first_slot, y_count, block_count, *refs):
    facts_ref, nope_ref, rotated_ref, up_ref = refs[:4]
    block_refs = refs[4 : 4 + block_count]
    highest_ref, totals_ref, mixed_ref, keys_ref, marks_ref = refs[-5:]

    @pl.when(pl.program_id(0) == 0)
    def _():
        fill_keys(
            facts_ref, block_refs, keys_ref, marks_ref, first_slot, y_count, nope_ref.shape[0]
        )

    results = attend(nope_ref, rotated_ref, up_ref, facts_ref, marks_ref, keys_ref, score_scale)
    for group, (highest, totals, mixed) in enumerate(results):
        highest_ref[group] = highest
        totals_ref[group] = totals
        mixed_ref[group] = mixed


def last_attention_kernel(score_scale, first_slot, y_count, block_count, *refs):
    facts_ref, nope_ref, rotated_ref, up_ref = refs[:4]
    block_refs = refs[4 : 4 + block_count]
    old_refs = refs[4 + block_count : 7 + block_count]
    proj_ref, hidden_ref, gain_ref = refs[7 + block_count : 10 + block_count]
    residual_ref, left_ref, right_ref, keys_ref, marks_ref, total_ref = refs[10 + block_count :]
    step = pl.program_id(0)
    rows = hidden_ref.shape[0]
    head_width = NOPE + VD

    @pl.when(step == 0)
    def _():
        fill_keys(facts_ref, block_refs, keys_ref, marks_ref, first_slot, y_count, rows)

    results = attend(nope_ref, rotated_ref, up_ref, facts_ref, marks_ref, keys_ref, score_scale)
    outs = []
    for group, result in enumerate(results):
        _, totals, mixed = merged(result, group, old_refs, score_scale)
        mixed = (mixed / totals).astype(jnp.bfloat16)
        for i in range(PAIR):
            head = group * PAIR + i
            outs.append(
                jnp.dot(
                    mixed[i * rows : (i + 1) * rows],
                    up_ref[:, head * head_width + NOPE : (head + 1) * head_width],
                    preferred_element_type=jnp.float32,
                ).astype(jnp.bfloat16)
            )
    head_out = jnp.concatenate(outs, axis=1)
    part = jnp.dot(head_out, proj_ref[...], preferred_element_type=jnp.float32)

    @pl.when(step == 0)
    def _():
        total_ref[...] = part

    @pl.when(step > 0)
    def _():
        total_ref[...] += part

    @pl.when(step == pl.num_programs(0) - 1)
    def _():
        residual = hidden_ref[...].astype(jnp.float32) + total_ref[...]
        residual_ref[...] = residual
        mean = jnp.mean(residual * residual, axis=1, keepdims=True)
        normed = (residual * lax.rsqrt(mean + epsilon) * gain_ref[...]).astype(jnp.bfloat16)
        left_ref[...] = normed[:, : left_ref.shape[1]]
        right_ref[...] = normed[:, left_ref.shape[1] :]


def attention_call(score_scale, first_slot, y_count, queries, blocks, old, tail, part=None):
    facts, nope, rotated, up = queries
    rows = nope.shape[0]
    latent_width = up.shape[0]
    block_height, width = blocks[0].shape
    keys = width * len(blocks)
    rotary_width = rotated.shape[2]
    heads = PAIR * GROUPS
    whole = lambda *shape: pl.BlockSpec(shape, lambda s: (0,) * len(shape))
    index, count = part or (0, 1)
    steps = H // heads // count
    start = index * steps
    state_specs = [
        pl.BlockSpec((GROUPS, PAIR * rows, size), lambda s: (s + start, 0, 0))
        for size in (1, 1, latent_width)
    ]
    in_specs = [
        pl.BlockSpec(memory_space=pltpu.SMEM),
        pl.BlockSpec((rows, heads * NOPE), lambda s: (0, s + start)),
        pl.BlockSpec((heads, rows, rotary_width), lambda s: (s + start, 0, 0)),
        pl.BlockSpec((latent_width, heads * (NOPE + VD)), lambda s: (0, s + start)),
    ] + [whole(block_height, width)] * len(blocks)
    scratch = [
        pltpu.VMEM((latent_width + rotary_width, keys), jnp.bfloat16),
        pltpu.VMEM((1, keys), jnp.int32),
    ]
    aliases = {}
    if old and part:
        aliases = {len(in_specs) + i: i for i in range(len(old))}
        in_specs += [pl.BlockSpec(memory_space=pl.ANY)] * len(old)
    elif old:
        in_specs += state_specs
    if tail:
        proj, hidden, gain = tail
        model_width = hidden.shape[1]
        kernel = last_attention_kernel
        in_specs += [
            pl.BlockSpec((heads * VD, model_width), lambda s: (s, 0)),
            whole(rows, model_width),
            whole(1, model_width),
        ]
        out_specs = [whole(rows, model_width)] + [whole(rows, model_width // 2)] * 2
        out_shape = [
            jax.ShapeDtypeStruct((rows, model_width), jnp.float32),
            jax.ShapeDtypeStruct((rows, model_width // 2), jnp.bfloat16),
            jax.ShapeDtypeStruct((rows, model_width // 2), jnp.bfloat16),
        ]
        scratch.append(pltpu.VMEM((rows, model_width), jnp.float32))
    else:
        kernel = first_attention_kernel
        out_specs = state_specs
        out_shape = [
            jax.ShapeDtypeStruct((H // PAIR, PAIR * rows, size), jnp.float32)
            for size in (1, 1, latent_width)
        ]
    return pl.pallas_call(
        functools.partial(kernel, score_scale, first_slot, y_count, len(blocks)),
        grid=(steps,),
        in_specs=in_specs,
        out_specs=out_specs,
        out_shape=out_shape,
        scratch_shapes=scratch,
        input_output_aliases=aliases,
        compiler_params=pltpu.CompilerParams(vmem_limit_bytes=28 * MIB),
        cost_estimate=pl.CostEstimate(
            flops=2 * H * rows * keys * (2 * latent_width + rotary_width) // count,
            bytes_accessed=16 * MIB // count,
            transcendentals=H * rows * keys // count,
        ),
    )(facts, nope, rotated, up, *blocks, *old, *tail)


def experts_kernel(slabs_each, sorting, x_ref, *refs):
    if sorting:
        take_ref, put_ref = refs[:2]
        refs = refs[2:]
    in_refs = refs[:PARTS]
    out_weight_refs = refs[PARTS : 2 * PARTS]
    result_ref = refs[2 * PARTS]
    rows_ref, total_ref = refs[2 * PARTS + 1 :]
    expert = pl.program_id(0)
    slab = pl.program_id(1)

    @pl.when(slab == 0)
    def _():
        if sorting:
            rows_ref[...] = jnp.dot(
                take_ref[0], x_ref[...], preferred_element_type=jnp.float32
            ).astype(jnp.bfloat16)
        else:
            rows_ref[...] = x_ref[...]

    depth = in_refs[0].shape[1]
    projected = None
    for index, in_ref in enumerate(in_refs):
        piece = jnp.dot(
            rows_ref[:, index * depth : (index + 1) * depth],
            in_ref[0],
            preferred_element_type=jnp.float32,
        )
        projected = piece if projected is None else projected + piece
    piece_half = out_weight_refs[0].shape[1]
    half = piece_half * PARTS
    active = (jax.nn.silu(projected[:, :half]) * projected[:, half:]).astype(jnp.bfloat16)
    part = None
    for index, out_weight_ref in enumerate(out_weight_refs):
        piece = jnp.dot(
            active[:, index * piece_half : (index + 1) * piece_half],
            out_weight_ref[0],
            preferred_element_type=jnp.float32,
        )
        part = piece if part is None else part + piece

    if slabs_each > 1:

        @pl.when(slab == 0)
        def _():
            total_ref[...] = part

    @pl.when(slab == slabs_each - 1)
    def _():
        value = part
        if slabs_each > 1:
            value = value + total_ref[...]
        value = value.astype(jnp.bfloat16)
        if sorting:
            value = jnp.dot(put_ref[0], value, preferred_element_type=jnp.float32).astype(
                jnp.bfloat16
            )

            @pl.when(expert == 0)
            def _():
                result_ref[...] = value

            @pl.when(expert > 0)
            def _():
                result_ref[...] += value
        else:
            result_ref[...] = value


def experts(x, expert_in, expert_out, experts_here, group):
    rows, width = x.shape
    slabs_each = expert_in.shape[0] // experts_here
    half = expert_out.shape[1]
    each = rows // experts_here
    sorting = experts_here > 1
    operands = [x]
    in_specs = [pl.BlockSpec((rows, width), lambda e, s: (0, 0))]
    if sorting:
        place = jnp.arange(each, dtype=jnp.int32)
        target = (
            (place // group * experts_here)[None, :]
            + jnp.arange(experts_here, dtype=jnp.int32)[:, None]
        ) * group + (place % group)[None, :]
        column = jnp.arange(rows, dtype=jnp.int32)
        take = (target[:, :, None] == column[None, None, :]).astype(jnp.bfloat16)
        put = (target[:, None, :] == column[None, :, None]).astype(jnp.bfloat16)
        operands += [take, put]
        in_specs += [
            pl.BlockSpec((1, each, rows), lambda e, s: (e, 0, 0)),
            pl.BlockSpec((1, rows, each), lambda e, s: (e, 0, 0)),
        ]

    def piece(height, columns, index):
        return pl.BlockSpec((1, height, columns), lambda e, s: (e * slabs_each + s, index, 0))

    operands += [expert_in] * PARTS + [expert_out] * PARTS
    in_specs += [piece(width // PARTS, 2 * half, i) for i in range(PARTS)]
    in_specs += [piece(half // PARTS, width, i) for i in range(PARTS)]
    return pl.pallas_call(
        functools.partial(experts_kernel, slabs_each, sorting),
        grid=(experts_here, slabs_each),
        in_specs=in_specs,
        out_specs=pl.BlockSpec((rows, width), lambda e, s: (0, 0)),
        out_shape=jax.ShapeDtypeStruct((rows, width), jnp.bfloat16),
        scratch_shapes=[
            pltpu.VMEM((each, width), jnp.bfloat16),
            pltpu.VMEM((each, width), jnp.float32),
        ],
        compiler_params=pltpu.CompilerParams(vmem_limit_bytes=44 * MIB),
        cost_estimate=pl.CostEstimate(
            flops=6 * rows * width * half * slabs_each,
            bytes_accessed=2 * 3 * width * half * experts_here * slabs_each,
            transcendentals=rows * half,
        ),
    )(*operands)


def pack_kernel(layers, place_ref, *refs):
    *token_refs, result_ref = refs
    sides = len(token_refs) // (2 * layers)
    width = token_refs[0].shape[1]
    for side in range(sides):
        blocks = []
        for block in range(2):
            value = None
            for layer in range(layers):
                piece = token_refs[(block * layers + layer) * sides + side][...]
                value = piece if value is None else value + piece
            blocks.append(value)
        tokens = jnp.concatenate(blocks, axis=0)
        result_ref[:, side * width : (side + 1) * width] = jnp.dot(
            place_ref[...], tokens, preferred_element_type=jnp.float32
        ).astype(jnp.bfloat16)


def pack(placing, blocks):
    layers = len(blocks[0])
    operands = [half for block in blocks for layer in block for half in layer]
    rows, tokens = placing.shape
    width = sum(half.shape[1] for half in blocks[0][0])
    return pl.pallas_call(
        functools.partial(pack_kernel, layers),
        out_shape=jax.ShapeDtypeStruct((rows, width), jnp.bfloat16),
        compiler_params=pltpu.CompilerParams(vmem_limit_bytes=24 * MIB),
        cost_estimate=pl.CostEstimate(
            flops=2 * rows * tokens * width, bytes_accessed=6 * rows * width, transcendentals=0
        ),
    )(placing, *operands)


def combine_kernel(weights_ref, rows_ref, *out_refs):
    value = jnp.dot(weights_ref[...], rows_ref[...], preferred_element_type=jnp.float32)
    row = 0
    column = 0
    for out_ref in out_refs:
        height, width = out_ref.shape
        out_ref[...] = value[row : row + height, column : column + width].astype(out_ref.dtype)
        column += width
        if column == value.shape[1]:
            row, column = row + height, 0


def combine(weights, rows, out_shape):
    return pl.pallas_call(
        combine_kernel,
        out_shape=out_shape,
        compiler_params=pltpu.CompilerParams(vmem_limit_bytes=24 * MIB),
        cost_estimate=pl.CostEstimate(
            flops=2 * weights.shape[0] * rows.size,
            bytes_accessed=4 * rows.size,
            transcendentals=0,
        ),
    )(weights, rows)


def finish_kernel(residual_ref, own_ref, *refs):
    *part_refs, out_ref = refs
    width = part_refs[0].shape[1]
    for side in range(2):
        columns = slice(side * width, (side + 1) * width)
        value = residual_ref[:, columns] + own_ref[:, columns]
        for part_ref in part_refs[side::2]:
            value = value + part_ref[...].astype(jnp.float32)
        out_ref[:, columns] = value.astype(out_ref.dtype)


def local(
    hidden,
    queries,
    fresh_latent,
    latent_cache,
    page_table,
    cache_lengths,
    routes,
    route_gates,
    kv_up,
    out_proj,
    latent_gain,
    norm_gain,
    expert_in,
    expert_out,
):
    row_count = hidden.shape[1]
    model_width = hidden.shape[2]
    latent_width = latent_gain.shape[0]
    entry_width = fresh_latent.shape[2]
    rotary_width = entry_width - latent_width
    half_rotary = rotary_width // 2
    score_scale = 1.0 / math.sqrt(NOPE + rotary_width)
    length = cache_lengths[0]
    y_count = lax.axis_size("y")
    z_index = lax.axis_index("z")
    y_index = lax.axis_index("y")
    tok_index = z_index * y_count + y_index
    tok_count = PLANES * y_count

    first_row = tok_index * row_count
    offsets = jnp.arange(row_count, dtype=jnp.int32)
    positions = (length + first_row + offsets).astype(jnp.float32)
    frequency = theta_base ** (-jnp.arange(half_rotary, dtype=jnp.float32) * 2.0 / rotary_width)
    angles = frequency[:, None] * positions[None, :]
    cosine = jnp.cos(angles)
    sine = jnp.sin(angles)
    page_size = latent_cache.shape[2]
    top_count = routes.shape[2]
    own_facts = jnp.concatenate(
        [
            routes[0].T.astype(jnp.bfloat16),
            route_gates[0].T.astype(jnp.bfloat16),
            jnp.zeros((FACT_ROWS - 2 * top_count, row_count), jnp.bfloat16),
        ],
        axis=0,
    )
    own_block, new_entries = pl.pallas_call(
        entries_kernel,
        out_shape=[
            jax.ShapeDtypeStruct((entry_width + FACT_ROWS, page_size + row_count), jnp.bfloat16),
            jax.ShapeDtypeStruct((entry_width, row_count), jnp.bfloat16),
        ],
    )(
        fresh_latent[0].T,
        latent_cache[0, 0].T,
        own_facts,
        cosine,
        sine,
        latent_gain.reshape(latent_width // row_count, row_count),
    )

    inner = jnp.logical_or(z_index == 1, z_index == 2)

    def along_z(values):
        near = lax.ppermute(values, "z", NEAR)
        middle = lax.ppermute(values, "z", MIDDLE)
        middle_far = lax.ppermute(near, "z", MIDDLE)
        outward = lax.ppermute(middle, "z", OUTWARD)
        outward_far = lax.ppermute(middle_far, "z", OUTWARD)
        return near, (middle, outward), (middle_far, outward_far)

    near_block, *far_blocks = along_z(own_block)
    z_blocks = [own_block, near_block] + [jnp.where(inner, *pair) for pair in far_blocks]
    blocks = [
        z_block if j == 0 else shifted(z_block, "y", j)
        for z_block in z_blocks
        for j in range(y_count)
    ]

    query_rows = queries[0].reshape(row_count, H, NOPE + rotary_width)
    nope = query_rows[:, :, :NOPE].reshape(row_count, H * NOPE)
    turning = query_rows[:, :, NOPE:].astype(jnp.float32).transpose(1, 0, 2)
    front, back = turning[:, :, :half_rotary], turning[:, :, half_rotary:]
    token_cosine, token_sine = cosine.T[None], sine.T[None]
    rotated = jnp.concatenate(
        [front * token_cosine - back * token_sine, back * token_cosine + front * token_sine],
        axis=2,
    ).astype(jnp.bfloat16)

    places = jnp.stack(
        [length, z_index.astype(jnp.int32), y_index.astype(jnp.int32), jnp.int32(y_count)]
    )
    prepared = (jnp.concatenate([places, page_table[0]]), nope, rotated, kv_up)
    early = 2 * y_count
    first_blocks = blocks[:early]
    state = attention_call(score_scale, 0, y_count, prepared, first_blocks, (), (), (0, 2))
    state, blocks[-y_count] = lax.optimization_barrier((state, blocks[-y_count]))
    state = attention_call(score_scale, 0, y_count, prepared, first_blocks, state, (), (1, 2))

    column_facts = [block[entry_width:, page_size:] for block in z_blocks]
    column_facts, state = lax.optimization_barrier((column_facts, state))
    residual, *normed = attention_call(
        score_scale,
        2,
        y_count,
        prepared,
        blocks[early:],
        state,
        (out_proj, hidden[0], norm_gain[None, :]),
    )

    slabs_here = expert_in.shape[0]
    experts_here = max(1, slabs_here // 2)
    x_count = lax.axis_size("x")
    plane_devices = x_count * 2 * y_count
    place = jnp.arange(plane_devices, dtype=jnp.int32)
    device_index = (place // y_count) * tok_count + z_index * y_count + place % y_count
    expert_ids = (
        (device_index * slabs_here)[:, None] // 2 + jnp.arange(experts_here, dtype=jnp.int32)
    ).reshape(-1)
    expert_ids = expert_ids.astype(jnp.float32)
    earlier = (offsets[:, None] < offsets[None, :]).astype(jnp.bfloat16)
    group = 2 * CAP
    expert_places = plane_devices * experts_here
    row_ids = jnp.arange(expert_places * group, dtype=jnp.int32)
    spread = (
        row_ids[:, None] // group == jnp.arange(expert_places, dtype=jnp.int32)[None, :]
    ).astype(jnp.bfloat16)
    wanted = (row_ids % group).astype(jnp.float32)[:, None]

    def pair_matrices(first, second):
        codes = []
        weights = []
        for index, fact in enumerate((first, second)):
            match = fact[None, :top_count, :].astype(jnp.float32) == expert_ids[:, None, None]
            named = jnp.any(match, axis=1)
            gates = fact[None, top_count : 2 * top_count, :].astype(jnp.float32)
            weights.append(jnp.sum(jnp.where(match, gates, 0.0), axis=1))
            rank = jnp.dot(
                named.astype(jnp.bfloat16), earlier, preferred_element_type=jnp.float32
            )
            codes.append(jnp.where(named, rank + index * CAP, -1.0))
        code = jnp.concatenate(codes, axis=1).astype(jnp.bfloat16)
        weight = jnp.concatenate(weights, axis=1).astype(jnp.bfloat16)
        chosen = jnp.dot(spread, code, preferred_element_type=jnp.float32) == wanted
        gate_rows = jnp.dot(spread, weight, preferred_element_type=jnp.float32)
        gate_rows = jnp.where(chosen, gate_rows, 0.0).astype(jnp.bfloat16)
        return chosen.astype(jnp.bfloat16), gate_rows.T

    near_matrices = pair_matrices(column_facts[0], column_facts[1])
    far_matrices = pair_matrices(column_facts[2], column_facts[3])

    def exchanged(values):
        return lax.all_to_all(values, PLANE_AXES, split_axis=0, concat_axis=0, tiled=True)

    def all_exchanged(rows):
        rows = rows.reshape(plane_devices, experts_here * group, model_width)
        return exchanged(rows).reshape(expert_places * group, model_width)

    near, *far = zip(*[along_z(half) for half in normed])
    (middle, outward), (other_middle, other_outward) = far[0]
    middle_far = far[1][0][0]
    near, middle, other_middle, outward, middle_far = lax.optimization_barrier(
        (near, middle, other_middle, outward, middle_far)
    )
    far[1] = [(middle_far, far[1][0][1]), far[1][1]]
    far[0] = [(middle, outward), (other_middle, other_outward)]
    near_rows = all_exchanged(pack(near_matrices[0], [[normed], [near]]))
    far = [list(zip(*block)) for block in far]
    near_rows, far = lax.optimization_barrier((near_rows, far))
    far_rows = all_exchanged(pack(far_matrices[0], far))
    near_rows = experts(near_rows, expert_in, expert_out, experts_here, group)
    near_rows, far_rows = lax.optimization_barrier((near_rows, far_rows))
    near_rows = all_exchanged(near_rows)
    far_rows = experts(far_rows, expert_in, expert_out, experts_here, group)
    near_rows, far_rows = lax.optimization_barrier((near_rows, far_rows))
    far_rows = all_exchanged(far_rows)

    def added(first, second):
        value = first.astype(jnp.float32) + second.astype(jnp.float32)
        return value.astype(jnp.bfloat16)

    def moved(value, pairs):
        return lax.ppermute(value, "z", pairs)

    half_shape = jax.ShapeDtypeStruct((row_count, model_width // 2), jnp.bfloat16)
    whole_shape = jax.ShapeDtypeStruct((row_count, model_width), jnp.float32)
    own_part, *near_parts = combine(
        near_matrices[1], near_rows, [whole_shape] + [half_shape] * 2
    )
    near_arrived = [moved(part, NEAR) for part in near_parts]
    near_arrived, far_rows = lax.optimization_barrier((near_arrived, far_rows))
    returned = combine(far_matrices[1], far_rows, [half_shape] * 4)
    middle_parts, far_parts = returned[:2], returned[2:]
    far_arrived = [moved(part, INWARD) for part in far_parts]
    middle_parts, far_arrived[1] = lax.optimization_barrier((middle_parts, far_arrived[1]))
    middle_arrived = [moved(part, INWARD) for part in middle_parts]
    far_arrived = [moved(added(*pair), MIDDLE) for pair in zip(far_parts, far_arrived)]
    middle_arrived = [moved(added(*pair), MIDDLE) for pair in zip(middle_parts, middle_arrived)]
    far_arrived = [moved(part, OUTWARD) for part in far_arrived]
    layer_out = pl.pallas_call(
        finish_kernel,
        out_shape=jax.ShapeDtypeStruct((row_count, model_width), jnp.bfloat16),
        compiler_params=pltpu.CompilerParams(vmem_limit_bytes=24 * MIB),
    )(residual, own_part, *near_arrived, *middle_arrived, *far_arrived)
    return (layer_out[None], new_entries.T[None])


def solution(mesh):
    req_count, tok_count = mesh.devices.shape
    devices = mesh.devices.reshape(req_count // 2, 2, PLANES, tok_count // PLANES)
    fine = Mesh(devices, ("x", "core", "z", "y"))
    req = ("x", "core")
    tok = ("z", "y")
    placed = (
        P(req, tok, None),
        P(req, tok, None),
        P(req, tok, None),
        P(req, tok, None, None),
        P(req, None),
        P(req),
        P(req, tok, None),
        P(req, tok, None),
        P(),
        P(),
        P(),
        P(),
        P(("x", "core", "z", "y"), None, None),
        P(("x", "core", "z", "y"), None, None),
    )
    return jax.shard_map(
        local,
        mesh=fine,
        in_specs=placed,
        out_specs=(P(req, tok, None), P(req, tok, None)),
        check_vma=False,
    )
```

```python
import functools
import math

import jax
import jax.numpy as jnp
from jax import lax
from jax.experimental import pallas as pl
from jax.experimental.pallas import tpu as pltpu
from jax.sharding import Mesh
from jax.sharding import PartitionSpec as P

H = 16
NOPE = 128
VD = 128
CAP = 14
PLANES = 4
PAIR = 2
GROUPS = 2
PARTS = 2

epsilon = 1e-06
theta_base = 10000.0
hidden_score = -1e30
PLANE_AXES = ("x", "core", "y")
MIB = 1 << 20
FACT_ROWS = 16
NEAR = [(0, 1), (1, 0), (2, 3), (3, 2)]
MIDDLE = [(1, 2), (2, 1)]
OUTWARD = [(1, 0), (2, 3)]
INWARD = [(0, 1), (3, 2)]


def shifted(values, axis, step):
    count = lax.axis_size(axis)
    return lax.ppermute(values, axis, [(i, (i + step) % count) for i in range(count)])


def entries_kernel(fresh_ref, page_ref, facts_ref, cos_ref, sin_ref, gain_ref, block_ref, new_ref):
    latent_width = gain_ref.shape[0] * gain_ref.shape[1]
    entry_width = fresh_ref.shape[0]
    half = cos_ref.shape[0]
    rows = fresh_ref.shape[1]
    raw = fresh_ref[:latent_width, :].astype(jnp.float32)
    mean = jnp.mean(raw * raw, axis=0, keepdims=True)
    gain = jnp.concatenate(
        [
            jnp.broadcast_to(gain_ref[i : i + 1, :], (rows, gain_ref.shape[1])).T
            for i in range(gain_ref.shape[0])
        ],
        axis=0,
    )
    latent = (raw * lax.rsqrt(mean + epsilon) * gain).astype(jnp.bfloat16)
    front = fresh_ref[latent_width : latent_width + half, :].astype(jnp.float32)
    back = fresh_ref[latent_width + half :, :].astype(jnp.float32)
    cosine = cos_ref[...]
    sine = sin_ref[...]
    turned_front = (front * cosine - back * sine).astype(jnp.bfloat16)
    turned_back = (back * cosine + front * sine).astype(jnp.bfloat16)
    new_ref[:latent_width, :] = latent
    new_ref[latent_width : latent_width + half, :] = turned_front
    new_ref[latent_width + half :, :] = turned_back
    block_ref[:entry_width, :rows] = page_ref[...]
    block_ref[:latent_width, rows:] = latent
    block_ref[latent_width : latent_width + half, rows:] = turned_front
    block_ref[latent_width + half : entry_width, rows:] = turned_back
    block_ref[entry_width:, rows:] = facts_ref[...]
    block_ref[entry_width:, :rows] = facts_ref[...]


def attend(nope_ref, rotated_ref, up_ref, facts_ref, marks_ref, keys_ref, values_ref, score_scale):
    latent_width = up_ref.shape[0]
    head_width = NOPE + VD
    keys_latent = keys_ref[:latent_width, :]
    keys_rotated = keys_ref[latent_width:, :]
    rows = nope_ref.shape[0]
    first_row = (facts_ref[1] * facts_ref[3] + facts_ref[2]) * rows
    query_rows = lax.broadcasted_iota(jnp.int32, (PAIR * rows, 1), 0)
    allowed = marks_ref[...] <= lax.rem(query_rows, rows) + first_row
    scores = []
    for group in range(GROUPS):
        heads = range(group * PAIR, (group + 1) * PAIR)
        query_latent = jnp.concatenate(
            [
                (
                    lax.dot_general(
                        nope_ref[:, i * NOPE : (i + 1) * NOPE],
                        up_ref[:, i * head_width : i * head_width + NOPE],
                        (((1,), (1,)), ((), ())),
                        preferred_element_type=jnp.float32,
                    )
                    * score_scale
                ).astype(jnp.bfloat16)
                for i in heads
            ],
            axis=0,
        )
        query_rotated = jnp.concatenate([rotated_ref[i] for i in heads], axis=0)
        value = jnp.dot(query_latent, keys_latent, preferred_element_type=jnp.float32)
        value = value + jnp.dot(query_rotated, keys_rotated, preferred_element_type=jnp.float32)
        scores.append(jnp.where(allowed, value, hidden_score))
    results = []
    for group in range(GROUPS):
        highest = jnp.max(scores[group], axis=1, keepdims=True)
        soft = jnp.exp2(scores[group] - highest)
        totals = jnp.sum(soft, axis=1, keepdims=True)
        mixed = jnp.dot(
            soft.astype(jnp.bfloat16), values_ref[...], preferred_element_type=jnp.float32
        )
        results.append((highest, totals, mixed))
    return results


def fill_keys(facts_ref, block_refs, keys_ref, values_ref, marks_ref, first_slot, y_count, rows):
    width = block_refs[0].shape[1]
    length, z_index, y_index = facts_ref[0], facts_ref[1], facts_ref[2]
    low = z_index < 2
    pool = facts_ref.shape[0] - 4
    page_size = width - rows
    for index, block_ref in enumerate(block_refs):
        keys_ref[:, index * width : (index + 1) * width] = block_ref[: keys_ref.shape[0], :]
        values_ref[index * width : (index + 1) * width, :] = block_ref[: values_ref.shape[1], :].T
        slot = first_slot + index // y_count
        z_source = (
            z_index,
            z_index + 1 - 2 * lax.rem(z_index, 2),
            jnp.where(low, 2, 1),
            jnp.where(low, 3, 0),
        )[slot]
        y_source = lax.rem(y_index + y_count - index % y_count, y_count)
        source = z_source * y_count + y_source
        logical = jnp.int32(0)
        for place in range(pool):
            logical = logical + jnp.where(facts_ref[4 + place] == source, place, 0)
        cached = lax.broadcasted_iota(jnp.int32, (1, page_size), 1) + logical * page_size
        marks_ref[:, index * width : index * width + page_size] = jnp.where(
            cached < length, -1, 1 << 30
        )
        marks_ref[:, index * width + page_size : (index + 1) * width] = (
            lax.broadcasted_iota(jnp.int32, (1, rows), 1) + source * rows
        )


def merged(result, group, old_refs):
    highest, totals, mixed = result
    old_highest, old_totals, old_mixed = [ref[group] for ref in old_refs]
    top = jnp.maximum(highest, old_highest)
    fresh = jnp.exp2(highest - top)
    fading = jnp.exp2(old_highest - top)
    return top, totals * fresh + old_totals * fading, mixed * fresh + old_mixed * fading


def first_attention_kernel(score_scale, first_slot, y_count, block_count, *refs):
    facts_ref, nope_ref, rotated_ref, up_ref = refs[:4]
    block_refs = refs[4 : 4 + block_count]
    highest_ref, totals_ref, mixed_ref, keys_ref, values_ref, marks_ref = refs[-6:]

    @pl.when(pl.program_id(0) == 0)
    def _():
        fill_keys(
            facts_ref,
            block_refs,
            keys_ref,
            values_ref,
            marks_ref,
            first_slot,
            y_count,
            nope_ref.shape[0],
        )

    results = attend(
        nope_ref, rotated_ref, up_ref, facts_ref, marks_ref, keys_ref, values_ref, score_scale
    )
    for group, (highest, totals, mixed) in enumerate(results):
        highest_ref[group] = highest
        totals_ref[group] = totals
        mixed_ref[group] = mixed


def last_attention_kernel(score_scale, first_slot, y_count, block_count, *refs):
    facts_ref, nope_ref, rotated_ref, up_ref = refs[:4]
    block_refs = refs[4 : 4 + block_count]
    old_refs = refs[4 + block_count : 7 + block_count]
    proj_ref, hidden_ref, gain_ref = refs[7 + block_count : 10 + block_count]
    residual_ref, left_ref, right_ref, keys_ref, values_ref, marks_ref, total_ref = refs[
        10 + block_count :
    ]
    step = pl.program_id(0)
    rows = hidden_ref.shape[0]
    head_width = NOPE + VD

    @pl.when(step == 0)
    def _():
        fill_keys(
            facts_ref, block_refs, keys_ref, values_ref, marks_ref, first_slot, y_count, rows
        )

    results = attend(
        nope_ref, rotated_ref, up_ref, facts_ref, marks_ref, keys_ref, values_ref, score_scale
    )
    outs = []
    for group, result in enumerate(results):
        _, totals, mixed = merged(result, group, old_refs)
        mixed = (mixed / totals).astype(jnp.bfloat16)
        for i in range(PAIR):
            head = group * PAIR + i
            outs.append(
                jnp.dot(
                    mixed[i * rows : (i + 1) * rows],
                    up_ref[:, head * head_width + NOPE : (head + 1) * head_width],
                    preferred_element_type=jnp.float32,
                ).astype(jnp.bfloat16)
            )
    head_out = jnp.concatenate(outs, axis=1)
    part = jnp.dot(head_out, proj_ref[...], preferred_element_type=jnp.float32)

    @pl.when(step == 0)
    def _():
        total_ref[...] = part

    @pl.when(step > 0)
    def _():
        total_ref[...] += part

    @pl.when(step == pl.num_programs(0) - 1)
    def _():
        residual = hidden_ref[...].astype(jnp.float32) + total_ref[...]
        residual_ref[...] = residual
        mean = jnp.mean(residual * residual, axis=1, keepdims=True)
        normed = (residual * lax.rsqrt(mean + epsilon) * gain_ref[...]).astype(jnp.bfloat16)
        left_ref[...] = normed[:, : left_ref.shape[1]]
        right_ref[...] = normed[:, left_ref.shape[1] :]


def attention_call(score_scale, first_slot, y_count, queries, blocks, old, tail, part=None):
    facts, nope, rotated, up = queries
    rows = nope.shape[0]
    latent_width = up.shape[0]
    block_height, width = blocks[0].shape
    keys = width * len(blocks)
    rotary_width = rotated.shape[2]
    heads = PAIR * GROUPS
    whole = lambda *shape: pl.BlockSpec(shape, lambda s: (0,) * len(shape))
    index, count = part or (0, 1)
    steps = H // heads // count
    start = index * steps
    state_specs = [
        pl.BlockSpec((GROUPS, PAIR * rows, size), lambda s: (s + start, 0, 0))
        for size in (1, 1, latent_width)
    ]
    in_specs = [
        pl.BlockSpec(memory_space=pltpu.SMEM),
        pl.BlockSpec((rows, heads * NOPE), lambda s: (0, s + start)),
        pl.BlockSpec((heads, rows, rotary_width), lambda s: (s + start, 0, 0)),
        pl.BlockSpec((latent_width, heads * (NOPE + VD)), lambda s: (0, s + start)),
    ] + [whole(block_height, width)] * len(blocks)
    scratch = [
        pltpu.VMEM((latent_width + rotary_width, keys), jnp.bfloat16),
        pltpu.VMEM((keys, latent_width), jnp.bfloat16),
        pltpu.VMEM((1, keys), jnp.int32),
    ]
    aliases = {}
    if old and part:
        aliases = {len(in_specs) + i: i for i in range(len(old))}
        in_specs += [pl.BlockSpec(memory_space=pl.ANY)] * len(old)
    elif old:
        in_specs += state_specs
    if tail:
        proj, hidden, gain = tail
        model_width = hidden.shape[1]
        kernel = last_attention_kernel
        in_specs += [
            pl.BlockSpec((heads * VD, model_width), lambda s: (s, 0)),
            whole(rows, model_width),
            whole(1, model_width),
        ]
        out_specs = [whole(rows, model_width)] + [whole(rows, model_width // 2)] * 2
        out_shape = [
            jax.ShapeDtypeStruct((rows, model_width), jnp.float32),
            jax.ShapeDtypeStruct((rows, model_width // 2), jnp.bfloat16),
            jax.ShapeDtypeStruct((rows, model_width // 2), jnp.bfloat16),
        ]
        scratch.append(pltpu.VMEM((rows, model_width), jnp.float32))
    else:
        kernel = first_attention_kernel
        out_specs = state_specs
        out_shape = [
            jax.ShapeDtypeStruct((H // PAIR, PAIR * rows, size), jnp.float32)
            for size in (1, 1, latent_width)
        ]
    return pl.pallas_call(
        functools.partial(kernel, score_scale, first_slot, y_count, len(blocks)),
        grid=(steps,),
        in_specs=in_specs,
        out_specs=out_specs,
        out_shape=out_shape,
        scratch_shapes=scratch,
        input_output_aliases=aliases,
        compiler_params=pltpu.CompilerParams(vmem_limit_bytes=28 * MIB),
        cost_estimate=pl.CostEstimate(
            flops=2 * H * rows * keys * (2 * latent_width + rotary_width) // count,
            bytes_accessed=16 * MIB // count,
            transcendentals=H * rows * keys // count,
        ),
    )(facts, nope, rotated, up, *blocks, *old, *tail)


def experts_kernel(slabs_each, sorting, x_ref, *refs):
    if sorting:
        take_ref, put_ref = refs[:2]
        refs = refs[2:]
    in_refs = refs[:PARTS]
    out_weight_refs = refs[PARTS : 2 * PARTS]
    result_ref = refs[2 * PARTS]
    rows_ref, total_ref = refs[2 * PARTS + 1 :]
    expert = pl.program_id(0)
    slab = pl.program_id(1)

    @pl.when(slab == 0)
    def _():
        if sorting:
            rows_ref[...] = jnp.dot(
                take_ref[0], x_ref[...], preferred_element_type=jnp.float32
            ).astype(jnp.bfloat16)
        else:
            rows_ref[...] = x_ref[...]

    depth = in_refs[0].shape[1]
    projected = None
    for index, in_ref in enumerate(in_refs):
        piece = jnp.dot(
            rows_ref[:, index * depth : (index + 1) * depth],
            in_ref[0],
            preferred_element_type=jnp.float32,
        )
        projected = piece if projected is None else projected + piece
    piece_half = out_weight_refs[0].shape[1]
    half = piece_half * PARTS
    active = (jax.nn.silu(projected[:, :half]) * projected[:, half:]).astype(jnp.bfloat16)
    part = None
    for index, out_weight_ref in enumerate(out_weight_refs):
        piece = jnp.dot(
            active[:, index * piece_half : (index + 1) * piece_half],
            out_weight_ref[0],
            preferred_element_type=jnp.float32,
        )
        part = piece if part is None else part + piece

    if slabs_each > 1:

        @pl.when(slab == 0)
        def _():
            total_ref[...] = part

    @pl.when(slab == slabs_each - 1)
    def _():
        value = part
        if slabs_each > 1:
            value = value + total_ref[...]
        value = value.astype(jnp.bfloat16)
        if sorting:
            value = jnp.dot(put_ref[0], value, preferred_element_type=jnp.float32).astype(
                jnp.bfloat16
            )

            @pl.when(expert == 0)
            def _():
                result_ref[...] = value

            @pl.when(expert > 0)
            def _():
                result_ref[...] += value
        else:
            result_ref[...] = value


def experts(x, expert_in, expert_out, experts_here, group):
    rows, width = x.shape
    slabs_each = expert_in.shape[0] // experts_here
    half = expert_out.shape[1]
    each = rows // experts_here
    sorting = experts_here > 1
    operands = [x]
    in_specs = [pl.BlockSpec((rows, width), lambda e, s: (0, 0))]
    if sorting:
        place = jnp.arange(each, dtype=jnp.int32)
        target = (
            (place // group * experts_here)[None, :]
            + jnp.arange(experts_here, dtype=jnp.int32)[:, None]
        ) * group + (place % group)[None, :]
        column = jnp.arange(rows, dtype=jnp.int32)
        take = (target[:, :, None] == column[None, None, :]).astype(jnp.bfloat16)
        put = (target[:, None, :] == column[None, :, None]).astype(jnp.bfloat16)
        operands += [take, put]
        in_specs += [
            pl.BlockSpec((1, each, rows), lambda e, s: (e, 0, 0)),
            pl.BlockSpec((1, rows, each), lambda e, s: (e, 0, 0)),
        ]

    def piece(height, columns, index):
        return pl.BlockSpec((1, height, columns), lambda e, s: (e * slabs_each + s, index, 0))

    operands += [expert_in] * PARTS + [expert_out] * PARTS
    in_specs += [piece(width // PARTS, 2 * half, i) for i in range(PARTS)]
    in_specs += [piece(half // PARTS, width, i) for i in range(PARTS)]
    return pl.pallas_call(
        functools.partial(experts_kernel, slabs_each, sorting),
        grid=(experts_here, slabs_each),
        in_specs=in_specs,
        out_specs=pl.BlockSpec((rows, width), lambda e, s: (0, 0)),
        out_shape=jax.ShapeDtypeStruct((rows, width), jnp.bfloat16),
        scratch_shapes=[
            pltpu.VMEM((each, width), jnp.bfloat16),
            pltpu.VMEM((each, width), jnp.float32),
        ],
        compiler_params=pltpu.CompilerParams(vmem_limit_bytes=44 * MIB),
        cost_estimate=pl.CostEstimate(
            flops=6 * rows * width * half * slabs_each,
            bytes_accessed=2 * 3 * width * half * experts_here * slabs_each,
            transcendentals=rows * half,
        ),
    )(*operands)


def pack_kernel(layers, place_ref, *refs):
    *token_refs, result_ref = refs
    sides = len(token_refs) // (2 * layers)
    width = token_refs[0].shape[1]
    for side in range(sides):
        blocks = []
        for block in range(2):
            value = None
            for layer in range(layers):
                piece = token_refs[(block * layers + layer) * sides + side][...]
                value = piece if value is None else value + piece
            blocks.append(value)
        tokens = jnp.concatenate(blocks, axis=0)
        result_ref[:, side * width : (side + 1) * width] = jnp.dot(
            place_ref[...], tokens, preferred_element_type=jnp.float32
        ).astype(jnp.bfloat16)


def pack(placing, blocks):
    layers = len(blocks[0])
    operands = [half for block in blocks for layer in block for half in layer]
    rows, tokens = placing.shape
    width = sum(half.shape[1] for half in blocks[0][0])
    return pl.pallas_call(
        functools.partial(pack_kernel, layers),
        out_shape=jax.ShapeDtypeStruct((rows, width), jnp.bfloat16),
        compiler_params=pltpu.CompilerParams(vmem_limit_bytes=24 * MIB),
        cost_estimate=pl.CostEstimate(
            flops=2 * rows * tokens * width, bytes_accessed=6 * rows * width, transcendentals=0
        ),
    )(placing, *operands)


def combine_kernel(weights_ref, rows_ref, *out_refs):
    value = jnp.dot(weights_ref[...], rows_ref[...], preferred_element_type=jnp.float32)
    row = 0
    column = 0
    for out_ref in out_refs:
        height, width = out_ref.shape
        out_ref[...] = value[row : row + height, column : column + width].astype(out_ref.dtype)
        column += width
        if column == value.shape[1]:
            row, column = row + height, 0


def combine(weights, rows, out_shape):
    return pl.pallas_call(
        combine_kernel,
        out_shape=out_shape,
        compiler_params=pltpu.CompilerParams(vmem_limit_bytes=24 * MIB),
        cost_estimate=pl.CostEstimate(
            flops=2 * weights.shape[0] * rows.size,
            bytes_accessed=4 * rows.size,
            transcendentals=0,
        ),
    )(weights, rows)


def finish_kernel(residual_ref, own_ref, *refs):
    *part_refs, out_ref = refs
    width = part_refs[0].shape[1]
    for side in range(2):
        columns = slice(side * width, (side + 1) * width)
        value = residual_ref[:, columns] + own_ref[:, columns]
        for part_ref in part_refs[side::2]:
            value = value + part_ref[...].astype(jnp.float32)
        out_ref[:, columns] = value.astype(out_ref.dtype)


def local(
    hidden,
    queries,
    fresh_latent,
    latent_cache,
    page_table,
    cache_lengths,
    routes,
    route_gates,
    kv_up,
    out_proj,
    latent_gain,
    norm_gain,
    expert_in,
    expert_out,
):
    row_count = hidden.shape[1]
    model_width = hidden.shape[2]
    latent_width = latent_gain.shape[0]
    entry_width = fresh_latent.shape[2]
    rotary_width = entry_width - latent_width
    half_rotary = rotary_width // 2
    score_scale = math.log2(math.e) / math.sqrt(NOPE + rotary_width)
    length = cache_lengths[0]
    y_count = lax.axis_size("y")
    z_index = lax.axis_index("z")
    y_index = lax.axis_index("y")
    tok_index = z_index * y_count + y_index
    tok_count = PLANES * y_count

    first_row = tok_index * row_count
    offsets = jnp.arange(row_count, dtype=jnp.int32)
    positions = (length + first_row + offsets).astype(jnp.float32)
    frequency = theta_base ** (-jnp.arange(half_rotary, dtype=jnp.float32) * 2.0 / rotary_width)
    angles = frequency[:, None] * positions[None, :]
    cosine = jnp.cos(angles)
    sine = jnp.sin(angles)
    page_size = latent_cache.shape[2]
    top_count = routes.shape[2]
    own_facts = jnp.concatenate(
        [
            routes[0].T.astype(jnp.bfloat16),
            route_gates[0].T.astype(jnp.bfloat16),
            jnp.zeros((FACT_ROWS - 2 * top_count, row_count), jnp.bfloat16),
        ],
        axis=0,
    )
    own_block, new_entries = pl.pallas_call(
        entries_kernel,
        out_shape=[
            jax.ShapeDtypeStruct((entry_width + FACT_ROWS, page_size + row_count), jnp.bfloat16),
            jax.ShapeDtypeStruct((entry_width, row_count), jnp.bfloat16),
        ],
    )(
        fresh_latent[0].T,
        latent_cache[0, 0].T,
        own_facts,
        cosine,
        sine,
        latent_gain.reshape(latent_width // row_count, row_count),
    )

    inner = jnp.logical_or(z_index == 1, z_index == 2)

    def along_z(values):
        near = lax.ppermute(values, "z", NEAR)
        middle = lax.ppermute(values, "z", MIDDLE)
        middle_far = lax.ppermute(near, "z", MIDDLE)
        outward = lax.ppermute(middle, "z", OUTWARD)
        outward_far = lax.ppermute(middle_far, "z", OUTWARD)
        return near, (middle, outward), (middle_far, outward_far)

    near_block, *far_blocks = along_z(own_block)
    z_blocks = [own_block, near_block] + [jnp.where(inner, *pair) for pair in far_blocks]
    blocks = [
        z_block if j == 0 else shifted(z_block, "y", j)
        for z_block in z_blocks
        for j in range(y_count)
    ]

    query_rows = queries[0].reshape(row_count, H, NOPE + rotary_width)
    nope = query_rows[:, :, :NOPE].reshape(row_count, H * NOPE)
    turning = query_rows[:, :, NOPE:].astype(jnp.float32).transpose(1, 0, 2)
    front, back = turning[:, :, :half_rotary], turning[:, :, half_rotary:]
    token_cosine, token_sine = cosine.T[None], sine.T[None]
    rotated = (score_scale * jnp.concatenate(
        [front * token_cosine - back * token_sine, back * token_cosine + front * token_sine],
        axis=2,
    )).astype(jnp.bfloat16)

    places = jnp.stack(
        [length, z_index.astype(jnp.int32), y_index.astype(jnp.int32), jnp.int32(y_count)]
    )
    prepared = (jnp.concatenate([places, page_table[0]]), nope, rotated, kv_up)
    early = 2 * y_count
    first_blocks = blocks[:early]
    state = attention_call(score_scale, 0, y_count, prepared, first_blocks, (), (), (0, 2))
    state, blocks[-y_count] = lax.optimization_barrier((state, blocks[-y_count]))
    state = attention_call(score_scale, 0, y_count, prepared, first_blocks, state, (), (1, 2))

    column_facts = [block[entry_width:, page_size:] for block in z_blocks]
    column_facts, state = lax.optimization_barrier((column_facts, state))
    residual, *normed = attention_call(
        score_scale,
        2,
        y_count,
        prepared,
        blocks[early:],
        state,
        (out_proj, hidden[0], norm_gain[None, :]),
    )

    slabs_here = expert_in.shape[0]
    experts_here = max(1, slabs_here // 2)
    x_count = lax.axis_size("x")
    plane_devices = x_count * 2 * y_count
    place = jnp.arange(plane_devices, dtype=jnp.int32)
    device_index = (place // y_count) * tok_count + z_index * y_count + place % y_count
    expert_ids = (
        (device_index * slabs_here)[:, None] // 2 + jnp.arange(experts_here, dtype=jnp.int32)
    ).reshape(-1)
    expert_ids = expert_ids.astype(jnp.float32)
    earlier = (offsets[:, None] < offsets[None, :]).astype(jnp.bfloat16)
    group = 2 * CAP
    expert_places = plane_devices * experts_here
    row_ids = jnp.arange(expert_places * group, dtype=jnp.int32)
    spread = (
        row_ids[:, None] // group == jnp.arange(expert_places, dtype=jnp.int32)[None, :]
    ).astype(jnp.bfloat16)
    wanted = (row_ids % group).astype(jnp.float32)[:, None]

    def pair_matrices(first, second):
        codes = []
        weights = []
        for index, fact in enumerate((first, second)):
            match = fact[None, :top_count, :].astype(jnp.float32) == expert_ids[:, None, None]
            named = jnp.any(match, axis=1)
            gates = fact[None, top_count : 2 * top_count, :].astype(jnp.float32)
            weights.append(jnp.sum(jnp.where(match, gates, 0.0), axis=1))
            rank = jnp.dot(
                named.astype(jnp.bfloat16), earlier, preferred_element_type=jnp.float32
            )
            codes.append(jnp.where(named, rank + index * CAP, -1.0))
        code = jnp.concatenate(codes, axis=1).astype(jnp.bfloat16)
        weight = jnp.concatenate(weights, axis=1).astype(jnp.bfloat16)
        chosen = jnp.dot(spread, code, preferred_element_type=jnp.float32) == wanted
        gate_rows = jnp.dot(spread, weight, preferred_element_type=jnp.float32)
        gate_rows = jnp.where(chosen, gate_rows, 0.0).astype(jnp.bfloat16)
        return chosen.astype(jnp.bfloat16), gate_rows.T

    near_matrices = pair_matrices(column_facts[0], column_facts[1])
    far_matrices = pair_matrices(column_facts[2], column_facts[3])

    def exchanged(values):
        return lax.all_to_all(values, PLANE_AXES, split_axis=0, concat_axis=0, tiled=True)

    def all_exchanged(rows):
        rows = rows.reshape(plane_devices, experts_here * group, model_width)
        return exchanged(rows).reshape(expert_places * group, model_width)

    near, *far = zip(*[along_z(half) for half in normed])
    (middle, outward), (other_middle, other_outward) = far[0]
    middle_far = far[1][0][0]
    near, middle, other_middle, outward, middle_far = lax.optimization_barrier(
        (near, middle, other_middle, outward, middle_far)
    )
    far[1] = [(middle_far, far[1][0][1]), far[1][1]]
    far[0] = [(middle, outward), (other_middle, other_outward)]
    near_rows = all_exchanged(pack(near_matrices[0], [[normed], [near]]))
    far = [list(zip(*block)) for block in far]
    near_rows, far = lax.optimization_barrier((near_rows, far))
    far_rows = all_exchanged(pack(far_matrices[0], far))
    near_rows = experts(near_rows, expert_in, expert_out, experts_here, group)
    near_rows, far_rows = lax.optimization_barrier((near_rows, far_rows))
    near_rows = all_exchanged(near_rows)
    far_rows = experts(far_rows, expert_in, expert_out, experts_here, group)
    near_rows, far_rows = lax.optimization_barrier((near_rows, far_rows))
    far_rows = all_exchanged(far_rows)

    def added(first, second):
        value = first.astype(jnp.float32) + second.astype(jnp.float32)
        return value.astype(jnp.bfloat16)

    def moved(value, pairs):
        return lax.ppermute(value, "z", pairs)

    half_shape = jax.ShapeDtypeStruct((row_count, model_width // 2), jnp.bfloat16)
    whole_shape = jax.ShapeDtypeStruct((row_count, model_width), jnp.float32)
    own_part, *near_parts = combine(
        near_matrices[1], near_rows, [whole_shape] + [half_shape] * 2
    )
    near_arrived = [moved(part, NEAR) for part in near_parts]
    near_arrived, far_rows = lax.optimization_barrier((near_arrived, far_rows))
    returned = combine(far_matrices[1], far_rows, [half_shape] * 4)
    middle_parts, far_parts = returned[:2], returned[2:]
    far_arrived = [moved(part, INWARD) for part in far_parts]
    middle_parts, far_arrived[1] = lax.optimization_barrier((middle_parts, far_arrived[1]))
    middle_arrived = [moved(part, INWARD) for part in middle_parts]
    far_arrived = [moved(added(*pair), MIDDLE) for pair in zip(far_parts, far_arrived)]
    middle_arrived = [moved(added(*pair), MIDDLE) for pair in zip(middle_parts, middle_arrived)]
    far_arrived = [moved(part, OUTWARD) for part in far_arrived]
    layer_out = pl.pallas_call(
        finish_kernel,
        out_shape=jax.ShapeDtypeStruct((row_count, model_width), jnp.bfloat16),
        compiler_params=pltpu.CompilerParams(vmem_limit_bytes=24 * MIB),
    )(residual, own_part, *near_arrived, *middle_arrived, *far_arrived)
    return (layer_out[None], new_entries.T[None])


def solution(mesh):
    req_count, tok_count = mesh.devices.shape
    devices = mesh.devices.reshape(req_count // 2, 2, PLANES, tok_count // PLANES)
    fine = Mesh(devices, ("x", "core", "z", "y"))
    req = ("x", "core")
    tok = ("z", "y")
    placed = (
        P(req, tok, None),
        P(req, tok, None),
        P(req, tok, None),
        P(req, tok, None, None),
        P(req, None),
        P(req),
        P(req, tok, None),
        P(req, tok, None),
        P(),
        P(),
        P(),
        P(),
        P(("x", "core", "z", "y"), None, None),
        P(("x", "core", "z", "y"), None, None),
    )
    return jax.shard_map(
        local,
        mesh=fine,
        in_specs=placed,
        out_specs=(P(req, tok, None), P(req, tok, None)),
        check_vma=False,
    )
```

```python
import functools
import math

import jax
import jax.numpy as jnp
from jax import lax
from jax.experimental import pallas as pl
from jax.experimental.pallas import tpu as pltpu
from jax.sharding import Mesh
from jax.sharding import PartitionSpec as P

H = 16
NOPE = 128
VD = 128
CAP = 14
PLANES = 4
PAIR = 2
GROUPS = 2
PARTS = 2

epsilon = 1e-06
theta_base = 10000.0
hidden_score = -1e30
PLANE_AXES = ("x", "core", "y")
MIB = 1 << 20
FACT_ROWS = 16
NEAR = [(0, 1), (1, 0), (2, 3), (3, 2)]
MIDDLE = [(1, 2), (2, 1)]
OUTWARD = [(1, 0), (2, 3)]
INWARD = [(0, 1), (3, 2)]


def shifted(values, axis, step):
    count = lax.axis_size(axis)
    return lax.ppermute(values, axis, [(i, (i + step) % count) for i in range(count)])


def entries_kernel(fresh_ref, page_ref, facts_ref, cos_ref, sin_ref, gain_ref, block_ref, new_ref):
    latent_width = gain_ref.shape[0] * gain_ref.shape[1]
    entry_width = fresh_ref.shape[0]
    half = cos_ref.shape[0]
    rows = fresh_ref.shape[1]
    raw = fresh_ref[:latent_width, :].astype(jnp.float32)
    mean = jnp.mean(raw * raw, axis=0, keepdims=True)
    gain = jnp.concatenate(
        [
            jnp.broadcast_to(gain_ref[i : i + 1, :], (rows, gain_ref.shape[1])).T
            for i in range(gain_ref.shape[0])
        ],
        axis=0,
    )
    latent = (raw * lax.rsqrt(mean + epsilon) * gain).astype(jnp.bfloat16)
    front = fresh_ref[latent_width : latent_width + half, :].astype(jnp.float32)
    back = fresh_ref[latent_width + half :, :].astype(jnp.float32)
    cosine = cos_ref[...]
    sine = sin_ref[...]
    turned_front = (front * cosine - back * sine).astype(jnp.bfloat16)
    turned_back = (back * cosine + front * sine).astype(jnp.bfloat16)
    new_ref[:latent_width, :] = latent
    new_ref[latent_width : latent_width + half, :] = turned_front
    new_ref[latent_width + half :, :] = turned_back
    block_ref[:entry_width, :rows] = page_ref[...]
    block_ref[:latent_width, rows:] = latent
    block_ref[latent_width : latent_width + half, rows:] = turned_front
    block_ref[latent_width + half : entry_width, rows:] = turned_back
    block_ref[entry_width:, rows:] = facts_ref[...]
    block_ref[entry_width:, :rows] = facts_ref[...]


def attend(nope_ref, rotated_ref, up_ref, facts_ref, marks_ref, keys_ref, score_scale):
    latent_width = up_ref.shape[0]
    head_width = NOPE + VD
    keys_latent = keys_ref[:latent_width, :]
    keys_rotated = keys_ref[latent_width:, :]
    rows = nope_ref.shape[0]
    first_row = (facts_ref[1] * facts_ref[3] + facts_ref[2]) * rows
    query_rows = lax.broadcasted_iota(jnp.int32, (PAIR * rows, 1), 0)
    allowed = marks_ref[...] <= lax.rem(query_rows, rows) + first_row
    scores = []
    for group in range(GROUPS):
        heads = range(group * PAIR, (group + 1) * PAIR)
        query_latent = jnp.concatenate(
            [
                lax.dot_general(
                    nope_ref[:, i * NOPE : (i + 1) * NOPE],
                    up_ref[:, i * head_width : i * head_width + NOPE],
                    (((1,), (1,)), ((), ())),
                    preferred_element_type=jnp.float32,
                ).astype(jnp.bfloat16)
                for i in heads
            ],
            axis=0,
        )
        query_rotated = jnp.concatenate([rotated_ref[i] for i in heads], axis=0)
        value = jnp.dot(query_latent, keys_latent, preferred_element_type=jnp.float32)
        value = value + jnp.dot(query_rotated, keys_rotated, preferred_element_type=jnp.float32)
        scores.append(jnp.where(allowed, value, hidden_score))
    results = []
    for group in range(GROUPS):
        highest = jnp.max(scores[group], axis=1, keepdims=True)
        soft = jnp.exp((scores[group] - highest) * score_scale)
        totals = jnp.sum(soft, axis=1, keepdims=True)
        mixed = lax.dot_general(
            soft.astype(jnp.bfloat16),
            keys_latent,
            (((1,), (1,)), ((), ())),
            preferred_element_type=jnp.float32,
        )
        results.append((highest, totals, mixed))
    return results


def fill_keys(facts_ref, block_refs, keys_ref, marks_ref, first_slot, y_count, rows):
    width = block_refs[0].shape[1]
    length, z_index, y_index = facts_ref[0], facts_ref[1], facts_ref[2]
    low = z_index < 2
    pool = facts_ref.shape[0] - 4
    page_size = width - rows
    for index, block_ref in enumerate(block_refs):
        keys_ref[:, index * width : (index + 1) * width] = block_ref[: keys_ref.shape[0], :]
        slot = first_slot + index // y_count
        z_source = (
            z_index,
            z_index + 1 - 2 * lax.rem(z_index, 2),
            jnp.where(low, 2, 1),
            jnp.where(low, 3, 0),
        )[slot]
        y_source = lax.rem(y_index + y_count - index % y_count, y_count)
        source = z_source * y_count + y_source
        logical = jnp.int32(0)
        for place in range(pool):
            logical = logical + jnp.where(facts_ref[4 + place] == source, place, 0)
        cached = lax.broadcasted_iota(jnp.int32, (1, page_size), 1) + logical * page_size
        marks_ref[:, index * width : index * width + page_size] = jnp.where(
            cached < length, -1, 1 << 30
        )
        marks_ref[:, index * width + page_size : (index + 1) * width] = (
            lax.broadcasted_iota(jnp.int32, (1, rows), 1) + source * rows
        )


def merged(result, group, old_refs, score_scale):
    highest, totals, mixed = result
    old_highest, old_totals, old_mixed = [ref[group] for ref in old_refs]
    top = jnp.maximum(highest, old_highest)
    fresh = jnp.exp((highest - top) * score_scale)
    fading = jnp.exp((old_highest - top) * score_scale)
    return top, totals * fresh + old_totals * fading, mixed * fresh + old_mixed * fading


def first_attention_kernel(score_scale, first_slot, y_count, block_count, *refs):
    facts_ref, nope_ref, rotated_ref, up_ref = refs[:4]
    block_refs = refs[4 : 4 + block_count]
    highest_ref, totals_ref, mixed_ref, keys_ref, marks_ref = refs[-5:]

    @pl.when(pl.program_id(0) == 0)
    def _():
        fill_keys(
            facts_ref, block_refs, keys_ref, marks_ref, first_slot, y_count, nope_ref.shape[0]
        )

    results = attend(nope_ref, rotated_ref, up_ref, facts_ref, marks_ref, keys_ref, score_scale)
    for group, (highest, totals, mixed) in enumerate(results):
        highest_ref[group] = highest
        totals_ref[group] = totals
        mixed_ref[group] = mixed


def last_attention_kernel(score_scale, first_slot, y_count, block_count, *refs):
    facts_ref, nope_ref, rotated_ref, up_ref = refs[:4]
    block_refs = refs[4 : 4 + block_count]
    old_refs = refs[4 + block_count : 7 + block_count]
    proj_ref, hidden_ref, gain_ref = refs[7 + block_count : 10 + block_count]
    residual_ref, left_ref, right_ref, keys_ref, marks_ref, total_ref = refs[10 + block_count :]
    step = pl.program_id(0)
    rows = hidden_ref.shape[0]
    head_width = NOPE + VD

    @pl.when(step == 0)
    def _():
        fill_keys(facts_ref, block_refs, keys_ref, marks_ref, first_slot, y_count, rows)

    results = attend(nope_ref, rotated_ref, up_ref, facts_ref, marks_ref, keys_ref, score_scale)
    outs = []
    for group, result in enumerate(results):
        _, totals, mixed = merged(result, group, old_refs, score_scale)
        mixed = (mixed / totals).astype(jnp.bfloat16)
        for i in range(PAIR):
            head = group * PAIR + i
            outs.append(
                jnp.dot(
                    mixed[i * rows : (i + 1) * rows],
                    up_ref[:, head * head_width + NOPE : (head + 1) * head_width],
                    preferred_element_type=jnp.float32,
                ).astype(jnp.bfloat16)
            )
    head_out = jnp.concatenate(outs, axis=1)
    part = jnp.dot(head_out, proj_ref[...], preferred_element_type=jnp.float32)

    @pl.when(step == 0)
    def _():
        total_ref[...] = part

    @pl.when(step > 0)
    def _():
        total_ref[...] += part

    @pl.when(step == pl.num_programs(0) - 1)
    def _():
        residual = hidden_ref[...].astype(jnp.float32) + total_ref[...]
        residual_ref[...] = residual
        mean = jnp.mean(residual * residual, axis=1, keepdims=True)
        normed = (residual * lax.rsqrt(mean + epsilon) * gain_ref[...]).astype(jnp.bfloat16)
        left_ref[...] = normed[:, : left_ref.shape[1]]
        right_ref[...] = normed[:, left_ref.shape[1] :]


def attention_call(score_scale, first_slot, y_count, queries, blocks, old, tail, part=None):
    facts, nope, rotated, up = queries
    rows = nope.shape[0]
    latent_width = up.shape[0]
    block_height, width = blocks[0].shape
    keys = width * len(blocks)
    rotary_width = rotated.shape[2]
    heads = PAIR * GROUPS
    whole = lambda *shape: pl.BlockSpec(shape, lambda s: (0,) * len(shape))
    index, count = part or (0, 1)
    steps = H // heads // count
    start = index * steps
    state_specs = [
        pl.BlockSpec((GROUPS, PAIR * rows, size), lambda s: (s + start, 0, 0))
        for size in (1, 1, latent_width)
    ]
    in_specs = [
        pl.BlockSpec(memory_space=pltpu.SMEM),
        pl.BlockSpec((rows, heads * NOPE), lambda s: (0, s + start)),
        pl.BlockSpec((heads, rows, rotary_width), lambda s: (s + start, 0, 0)),
        pl.BlockSpec((latent_width, heads * (NOPE + VD)), lambda s: (0, s + start)),
    ] + [whole(block_height, width)] * len(blocks)
    scratch = [
        pltpu.VMEM((latent_width + rotary_width, keys), jnp.bfloat16),
        pltpu.VMEM((1, keys), jnp.int32),
    ]
    aliases = {}
    if old and part:
        aliases = {len(in_specs) + i: i for i in range(len(old))}
        in_specs += [pl.BlockSpec(memory_space=pl.ANY)] * len(old)
    elif old:
        in_specs += state_specs
    if tail:
        proj, hidden, gain = tail
        model_width = hidden.shape[1]
        kernel = last_attention_kernel
        in_specs += [
            pl.BlockSpec((heads * VD, model_width), lambda s: (s, 0)),
            whole(rows, model_width),
            whole(1, model_width),
        ]
        out_specs = [whole(rows, model_width)] + [whole(rows, model_width // 2)] * 2
        out_shape = [
            jax.ShapeDtypeStruct((rows, model_width), jnp.float32),
            jax.ShapeDtypeStruct((rows, model_width // 2), jnp.bfloat16),
            jax.ShapeDtypeStruct((rows, model_width // 2), jnp.bfloat16),
        ]
        scratch.append(pltpu.VMEM((rows, model_width), jnp.float32))
    else:
        kernel = first_attention_kernel
        out_specs = state_specs
        out_shape = [
            jax.ShapeDtypeStruct((H // PAIR, PAIR * rows, size), jnp.float32)
            for size in (1, 1, latent_width)
        ]
    return pl.pallas_call(
        functools.partial(kernel, score_scale, first_slot, y_count, len(blocks)),
        grid=(steps,),
        in_specs=in_specs,
        out_specs=out_specs,
        out_shape=out_shape,
        scratch_shapes=scratch,
        input_output_aliases=aliases,
        compiler_params=pltpu.CompilerParams(vmem_limit_bytes=28 * MIB),
        cost_estimate=pl.CostEstimate(
            flops=2 * H * rows * keys * (2 * latent_width + rotary_width) // count,
            bytes_accessed=16 * MIB // count,
            transcendentals=H * rows * keys // count,
        ),
    )(facts, nope, rotated, up, *blocks, *old, *tail)


def experts_kernel(slabs_each, sorting, x_ref, *refs):
    if sorting:
        take_ref, put_ref = refs[:2]
        refs = refs[2:]
    in_refs = refs[:PARTS]
    out_weight_refs = refs[PARTS : 2 * PARTS]
    result_ref = refs[2 * PARTS]
    rows_ref, total_ref = refs[2 * PARTS + 1 :]
    expert = pl.program_id(0)
    slab = pl.program_id(1)

    @pl.when(slab == 0)
    def _():
        if sorting:
            rows_ref[...] = jnp.dot(
                take_ref[0], x_ref[...], preferred_element_type=jnp.float32
            ).astype(jnp.bfloat16)
        else:
            rows_ref[...] = x_ref[...]

    depth = in_refs[0].shape[1]
    projected = None
    for index, in_ref in enumerate(in_refs):
        piece = jnp.dot(
            rows_ref[:, index * depth : (index + 1) * depth],
            in_ref[0],
            preferred_element_type=jnp.float32,
        )
        projected = piece if projected is None else projected + piece
    piece_half = out_weight_refs[0].shape[1]
    half = piece_half * PARTS
    active = (jax.nn.silu(projected[:, :half]) * projected[:, half:]).astype(jnp.bfloat16)
    part = None
    for index, out_weight_ref in enumerate(out_weight_refs):
        piece = jnp.dot(
            active[:, index * piece_half : (index + 1) * piece_half],
            out_weight_ref[0],
            preferred_element_type=jnp.float32,
        )
        part = piece if part is None else part + piece

    if slabs_each > 1:

        @pl.when(slab == 0)
        def _():
            total_ref[...] = part

    @pl.when(slab == slabs_each - 1)
    def _():
        value = part
        if slabs_each > 1:
            value = value + total_ref[...]
        value = value.astype(jnp.bfloat16)
        if sorting:
            value = jnp.dot(put_ref[0], value, preferred_element_type=jnp.float32).astype(
                jnp.bfloat16
            )

            @pl.when(expert == 0)
            def _():
                result_ref[...] = value

            @pl.when(expert > 0)
            def _():
                result_ref[...] += value
        else:
            result_ref[...] = value


def experts(x, expert_in, expert_out, experts_here, group):
    rows, width = x.shape
    slabs_each = expert_in.shape[0] // experts_here
    half = expert_out.shape[1]
    each = rows // experts_here
    sorting = experts_here > 1
    operands = [x]
    in_specs = [pl.BlockSpec((rows, width), lambda e, s: (0, 0))]
    if sorting:
        place = jnp.arange(each, dtype=jnp.int32)
        target = (
            (place // group * experts_here)[None, :]
            + jnp.arange(experts_here, dtype=jnp.int32)[:, None]
        ) * group + (place % group)[None, :]
        column = jnp.arange(rows, dtype=jnp.int32)
        take = (target[:, :, None] == column[None, None, :]).astype(jnp.bfloat16)
        put = (target[:, None, :] == column[None, :, None]).astype(jnp.bfloat16)
        operands += [take, put]
        in_specs += [
            pl.BlockSpec((1, each, rows), lambda e, s: (e, 0, 0)),
            pl.BlockSpec((1, rows, each), lambda e, s: (e, 0, 0)),
        ]

    def piece(height, columns, index):
        return pl.BlockSpec((1, height, columns), lambda e, s: (e * slabs_each + s, index, 0))

    operands += [expert_in] * PARTS + [expert_out] * PARTS
    in_specs += [piece(width // PARTS, 2 * half, i) for i in range(PARTS)]
    in_specs += [piece(half // PARTS, width, i) for i in range(PARTS)]
    return pl.pallas_call(
        functools.partial(experts_kernel, slabs_each, sorting),
        grid=(experts_here, slabs_each),
        in_specs=in_specs,
        out_specs=pl.BlockSpec((rows, width), lambda e, s: (0, 0)),
        out_shape=jax.ShapeDtypeStruct((rows, width), jnp.bfloat16),
        scratch_shapes=[
            pltpu.VMEM((each, width), jnp.bfloat16),
            pltpu.VMEM((each, width), jnp.float32),
        ],
        compiler_params=pltpu.CompilerParams(vmem_limit_bytes=36 * MIB),
        cost_estimate=pl.CostEstimate(
            flops=6 * rows * width * half * slabs_each,
            bytes_accessed=2 * 3 * width * half * experts_here * slabs_each,
            transcendentals=rows * half,
        ),
    )(*operands)


def pack_kernel(layers, place_ref, *refs):
    *token_refs, result_ref = refs
    sides = len(token_refs) // (2 * layers)
    width = token_refs[0].shape[1]
    for side in range(sides):
        blocks = []
        for block in range(2):
            value = None
            for layer in range(layers):
                piece = token_refs[(block * layers + layer) * sides + side][...]
                value = piece if value is None else value + piece
            blocks.append(value)
        tokens = jnp.concatenate(blocks, axis=0)
        result_ref[:, side * width : (side + 1) * width] = jnp.dot(
            place_ref[...], tokens, preferred_element_type=jnp.float32
        ).astype(jnp.bfloat16)


def pack(placing, blocks):
    layers = len(blocks[0])
    operands = [half for block in blocks for layer in block for half in layer]
    rows, tokens = placing.shape
    width = sum(half.shape[1] for half in blocks[0][0])
    return pl.pallas_call(
        functools.partial(pack_kernel, layers),
        out_shape=jax.ShapeDtypeStruct((rows, width), jnp.bfloat16),
        compiler_params=pltpu.CompilerParams(vmem_limit_bytes=16 * MIB),
        cost_estimate=pl.CostEstimate(
            flops=2 * rows * tokens * width, bytes_accessed=6 * rows * width, transcendentals=0
        ),
    )(placing, *operands)


def combine_kernel(weights_ref, rows_ref, *out_refs):
    value = jnp.dot(weights_ref[...], rows_ref[...], preferred_element_type=jnp.float32)
    row = 0
    column = 0
    for out_ref in out_refs:
        height, width = out_ref.shape
        out_ref[...] = value[row : row + height, column : column + width].astype(out_ref.dtype)
        column += width
        if column == value.shape[1]:
            row, column = row + height, 0


def combine(weights, rows, out_shape):
    return pl.pallas_call(
        combine_kernel,
        out_shape=out_shape,
        compiler_params=pltpu.CompilerParams(vmem_limit_bytes=16 * MIB),
        cost_estimate=pl.CostEstimate(
            flops=2 * weights.shape[0] * rows.size,
            bytes_accessed=4 * rows.size,
            transcendentals=0,
        ),
    )(weights, rows)


def finish_kernel(residual_ref, own_ref, *refs):
    *part_refs, out_ref = refs
    width = part_refs[0].shape[1]
    for side in range(2):
        columns = slice(side * width, (side + 1) * width)
        value = residual_ref[:, columns] + own_ref[:, columns]
        for part_ref in part_refs[side::2]:
            value = value + part_ref[...].astype(jnp.float32)
        out_ref[:, columns] = value.astype(out_ref.dtype)


def local(
    hidden,
    queries,
    fresh_latent,
    latent_cache,
    page_table,
    cache_lengths,
    routes,
    route_gates,
    kv_up,
    out_proj,
    latent_gain,
    norm_gain,
    expert_in,
    expert_out,
):
    row_count = hidden.shape[1]
    model_width = hidden.shape[2]
    latent_width = latent_gain.shape[0]
    entry_width = fresh_latent.shape[2]
    rotary_width = entry_width - latent_width
    half_rotary = rotary_width // 2
    score_scale = 1.0 / math.sqrt(NOPE + rotary_width)
    length = cache_lengths[0]
    y_count = lax.axis_size("y")
    z_index = lax.axis_index("z")
    y_index = lax.axis_index("y")
    tok_index = z_index * y_count + y_index
    tok_count = PLANES * y_count

    first_row = tok_index * row_count
    offsets = jnp.arange(row_count, dtype=jnp.int32)
    positions = (length + first_row + offsets).astype(jnp.float32)
    frequency = theta_base ** (-jnp.arange(half_rotary, dtype=jnp.float32) * 2.0 / rotary_width)
    angles = frequency[:, None] * positions[None, :]
    cosine = jnp.cos(angles)
    sine = jnp.sin(angles)
    page_size = latent_cache.shape[2]
    top_count = routes.shape[2]
    own_facts = jnp.concatenate(
        [
            routes[0].T.astype(jnp.bfloat16),
            route_gates[0].T.astype(jnp.bfloat16),
            jnp.zeros((FACT_ROWS - 2 * top_count, row_count), jnp.bfloat16),
        ],
        axis=0,
    )
    own_block, new_entries = pl.pallas_call(
        entries_kernel,
        out_shape=[
            jax.ShapeDtypeStruct((entry_width + FACT_ROWS, page_size + row_count), jnp.bfloat16),
            jax.ShapeDtypeStruct((entry_width, row_count), jnp.bfloat16),
        ],
    )(
        fresh_latent[0].T,
        latent_cache[0, 0].T,
        own_facts,
        cosine,
        sine,
        latent_gain.reshape(latent_width // row_count, row_count),
    )

    inner = jnp.logical_or(z_index == 1, z_index == 2)

    def along_z(values):
        near = lax.ppermute(values, "z", NEAR)
        middle = lax.ppermute(values, "z", MIDDLE)
        middle_far = lax.ppermute(near, "z", MIDDLE)
        outward = lax.ppermute(middle, "z", OUTWARD)
        outward_far = lax.ppermute(middle_far, "z", OUTWARD)
        return near, (middle, outward), (middle_far, outward_far)

    near_block, *far_blocks = along_z(own_block)
    z_blocks = [own_block, near_block] + [jnp.where(inner, *pair) for pair in far_blocks]
    blocks = [
        z_block if j == 0 else shifted(z_block, "y", j)
        for z_block in z_blocks
        for j in range(y_count)
    ]

    query_rows = queries[0].reshape(row_count, H, NOPE + rotary_width)
    nope = query_rows[:, :, :NOPE].reshape(row_count, H * NOPE)
    turning = query_rows[:, :, NOPE:].astype(jnp.float32).transpose(1, 0, 2)
    front, back = turning[:, :, :half_rotary], turning[:, :, half_rotary:]
    token_cosine, token_sine = cosine.T[None], sine.T[None]
    rotated = jnp.concatenate(
        [front * token_cosine - back * token_sine, back * token_cosine + front * token_sine],
        axis=2,
    ).astype(jnp.bfloat16)

    places = jnp.stack(
        [length, z_index.astype(jnp.int32), y_index.astype(jnp.int32), jnp.int32(y_count)]
    )
    prepared = (jnp.concatenate([places, page_table[0]]), nope, rotated, kv_up)
    early = 2 * y_count
    first_blocks = blocks[:early]
    state = attention_call(score_scale, 0, y_count, prepared, first_blocks, (), (), (0, 2))
    state, blocks[-y_count] = lax.optimization_barrier((state, blocks[-y_count]))
    state = attention_call(score_scale, 0, y_count, prepared, first_blocks, state, (), (1, 2))

    column_facts = [block[entry_width:, page_size:] for block in z_blocks]
    column_facts, state = lax.optimization_barrier((column_facts, state))
    residual, *normed = attention_call(
        score_scale,
        2,
        y_count,
        prepared,
        blocks[early:],
        state,
        (out_proj, hidden[0], norm_gain[None, :]),
    )

    slabs_here = expert_in.shape[0]
    experts_here = max(1, slabs_here // 2)
    x_count = lax.axis_size("x")
    plane_devices = x_count * 2 * y_count
    place = jnp.arange(plane_devices, dtype=jnp.int32)
    device_index = (place // y_count) * tok_count + z_index * y_count + place % y_count
    expert_ids = (
        (device_index * slabs_here)[:, None] // 2 + jnp.arange(experts_here, dtype=jnp.int32)
    ).reshape(-1)
    expert_ids = expert_ids.astype(jnp.float32)
    earlier = (offsets[:, None] < offsets[None, :]).astype(jnp.bfloat16)
    group = 2 * CAP
    expert_places = plane_devices * experts_here
    row_ids = jnp.arange(expert_places * group, dtype=jnp.int32)
    spread = (
        row_ids[:, None] // group == jnp.arange(expert_places, dtype=jnp.int32)[None, :]
    ).astype(jnp.bfloat16)
    wanted = (row_ids % group).astype(jnp.float32)[:, None]

    def pair_matrices(first, second):
        codes = []
        weights = []
        for index, fact in enumerate((first, second)):
            match = fact[None, :top_count, :].astype(jnp.float32) == expert_ids[:, None, None]
            named = jnp.any(match, axis=1)
            gates = fact[None, top_count : 2 * top_count, :].astype(jnp.float32)
            weights.append(jnp.sum(jnp.where(match, gates, 0.0), axis=1))
            rank = jnp.dot(
                named.astype(jnp.bfloat16), earlier, preferred_element_type=jnp.float32
            )
            codes.append(jnp.where(named, rank + index * CAP, -1.0))
        code = jnp.concatenate(codes, axis=1).astype(jnp.bfloat16)
        weight = jnp.concatenate(weights, axis=1).astype(jnp.bfloat16)
        chosen = jnp.dot(spread, code, preferred_element_type=jnp.float32) == wanted
        gate_rows = jnp.dot(spread, weight, preferred_element_type=jnp.float32)
        gate_rows = jnp.where(chosen, gate_rows, 0.0).astype(jnp.bfloat16)
        return chosen.astype(jnp.bfloat16), gate_rows.T

    near_matrices = pair_matrices(column_facts[0], column_facts[1])
    far_matrices = pair_matrices(column_facts[2], column_facts[3])

    def exchanged(values):
        return lax.all_to_all(values, PLANE_AXES, split_axis=0, concat_axis=0, tiled=True)

    def all_exchanged(rows):
        rows = rows.reshape(plane_devices, experts_here * group, model_width)
        return exchanged(rows).reshape(expert_places * group, model_width)

    near, *far = zip(*[along_z(half) for half in normed])
    (middle, outward), (other_middle, other_outward) = far[0]
    middle_far = far[1][0][0]
    near, middle, other_middle, outward, middle_far = lax.optimization_barrier(
        (near, middle, other_middle, outward, middle_far)
    )
    far[1] = [(middle_far, far[1][0][1]), far[1][1]]
    far[0] = [(middle, outward), (other_middle, other_outward)]
    near_rows = all_exchanged(pack(near_matrices[0], [[normed], [near]]))
    far = [list(zip(*block)) for block in far]
    near_rows, far = lax.optimization_barrier((near_rows, far))
    far_rows = all_exchanged(pack(far_matrices[0], far))
    near_rows = experts(near_rows, expert_in, expert_out, experts_here, group)
    near_rows, far_rows = lax.optimization_barrier((near_rows, far_rows))
    near_rows = all_exchanged(near_rows)
    far_rows = experts(far_rows, expert_in, expert_out, experts_here, group)
    near_rows, far_rows = lax.optimization_barrier((near_rows, far_rows))
    far_rows = all_exchanged(far_rows)

    def added(first, second):
        value = first.astype(jnp.float32) + second.astype(jnp.float32)
        return value.astype(jnp.bfloat16)

    def moved(value, pairs):
        return lax.ppermute(value, "z", pairs)

    half_shape = jax.ShapeDtypeStruct((row_count, model_width // 2), jnp.bfloat16)
    whole_shape = jax.ShapeDtypeStruct((row_count, model_width), jnp.float32)
    own_part, *near_parts = combine(
        near_matrices[1], near_rows, [whole_shape] + [half_shape] * 2
    )
    near_arrived = [moved(part, NEAR) for part in near_parts]
    near_arrived, far_rows = lax.optimization_barrier((near_arrived, far_rows))
    returned = combine(far_matrices[1], far_rows, [half_shape] * 4)
    middle_parts, far_parts = returned[:2], returned[2:]
    far_arrived = [moved(part, INWARD) for part in far_parts]
    middle_parts, far_arrived[1] = lax.optimization_barrier((middle_parts, far_arrived[1]))
    middle_arrived = [moved(part, INWARD) for part in middle_parts]
    far_arrived = [moved(added(*pair), MIDDLE) for pair in zip(far_parts, far_arrived)]
    middle_arrived = [moved(added(*pair), MIDDLE) for pair in zip(middle_parts, middle_arrived)]
    far_arrived = [moved(part, OUTWARD) for part in far_arrived]
    layer_out = pl.pallas_call(
        finish_kernel,
        out_shape=jax.ShapeDtypeStruct((row_count, model_width), jnp.bfloat16),
        compiler_params=pltpu.CompilerParams(vmem_limit_bytes=16 * MIB),
    )(residual, own_part, *near_arrived, *middle_arrived, *far_arrived)
    return (layer_out[None], new_entries.T[None])


def solution(mesh):
    req_count, tok_count = mesh.devices.shape
    devices = mesh.devices.reshape(req_count // 2, 2, PLANES, tok_count // PLANES)
    fine = Mesh(devices, ("x", "core", "z", "y"))
    req = ("x", "core")
    tok = ("z", "y")
    placed = (
        P(req, tok, None),
        P(req, tok, None),
        P(req, tok, None),
        P(req, tok, None, None),
        P(req, None),
        P(req),
        P(req, tok, None),
        P(req, tok, None),
        P(),
        P(),
        P(),
        P(),
        P(("x", "core", "z", "y"), None, None),
        P(("x", "core", "z", "y"), None, None),
    )
    return jax.shard_map(
        local,
        mesh=fine,
        in_specs=placed,
        out_specs=(P(req, tok, None), P(req, tok, None)),
        check_vma=False,
    )
```
